32 devices in a mesh: row: 4 (over y, x), col: 8 (over z, core).
Axes of the slice: x: 2, y: 2, z: 4, core: 2. Of those that a mesh axis runs over, the one named last changes fastest.
Arguments:
- flexibility: float32 [4, 8, 5, 1024, 1024], P('row', 'col'), as said below
- coupling: float32 [4, 8, 5, 24, 1024], P('row', 'col'), may hold values from -0.75 to 0.75
- coarse_inverse: float32 [1536, 1536], P(('row', 'col')), as said below
- precon_weight: float32 [4, 8, 5, 4, 128], P('row', 'col'), may hold values from 0.25 to 2
- right_side: float32 [4, 8, 5, 16, 4, 128], P('row', 'col'), may hold values from -6 to 6
- counts: int32 [4, 8], P('row', 'col'), may hold values from 2 to 5, as said below
- partner: int32 [4, 8, 4, 5], P('row', 'col'), may hold values from 0 to 4, each once within a row
- dof_index: int32 [4, 8, 5, 4, 128], P('row', 'col'), may hold values from 0 to 127, each once within a row
- corner_map: int32 [4, 8, 5, 24], P('row', 'col'), may hold values from 0 to 1535
Outputs:
- solution: float32 [4, 8, 5, 16, 4, 128], P('row', 'col')
- residual: float32 [4, 8, 5, 16, 4, 128], P('row', 'col')
The draws below stay inside these ranges and needn't reach their ends.
Inputs may be any that keep to these rules, and one draw needn't show every extreme that they name: A device's live subdomains are its first counts slots; some device has 5 and some device has 2 in every draw. `partner`: for each device and each link block separately, the 5 entries are a permutation of the slots; the same values recur on other devices, link blocks and device rows. `dof_index`: for each device, slot and link block separately, the 128 entries are a permutation of the block's unknowns; the same values recur on other slots, link blocks, devices and device rows. `flexibility`: symmetric positive definite. `coarse_inverse`: symmetric positive definite.
All inputs are finite; a program needn't handle non-finite values.
Results may differ from the reference program's by a relative error of at most 0.00029.
Values sent between devices are 32-bit elements; how exact they have to be, the bound alone decides.
No kernel may reach another device: no remote copies, remote signals or barrier semaphores. Data moves between devices by JAX's collectives and lax.ppermute only.
A program may use at most 128 MiB of HBM per device.

```python
import math
import jax
import jax.numpy as jnp
from jax import lax

IFACE = 1024
LINKS = 4
PAIR = 128
NCOR = 24
SLOTS = 5
NC = 1536
LOADS = 16
ITERS = 3
N_ROW = 4
N_COL = 8


def dominant_matrix(key, shape, order, low, high, spread):
    key_off, key_diag = jax.random.split(key, 2)
    offdiag = jax.random.uniform(key_off, shape, jnp.float32, -1.0, 1.0) * (spread * order ** (-0.5))
    offdiag = (offdiag + jnp.swapaxes(offdiag, -1, -2)) * 0.5
    diag_vals = jax.random.uniform(key_diag, shape[:-1], jnp.float32, low, high)
    ident = (jnp.arange(order)[:, None] == jnp.arange(order)[None, :]).astype(jnp.float32)
    matrix = offdiag * (1.0 - ident) + ident * diag_vals[..., None, :]
    return matrix


def draw_flexibility(key, part):
    return dominant_matrix(jax.random.fold_in(key, 11), (N_ROW, N_COL, SLOTS, IFACE, IFACE), IFACE, 1.5, 3.0, 1.2)


def draw_coarse_inverse(key, part):
    return dominant_matrix(jax.random.fold_in(key, 12), (NC, NC), NC, 1.0, 2.0, 0.9)


def draw_counts(key, part):
    key_main, key_high, key_low = jax.random.split(jax.random.fold_in(key, 13), 3)
    total = N_ROW * N_COL
    flat = jax.random.randint(key_main, (total,), 2, SLOTS + 1)
    high_at = jax.random.randint(key_high, (), 0, total)
    low_at = (high_at + 1 + jax.random.randint(key_low, (), 0, total - 1)) % total
    flat = flat.at[high_at].set(SLOTS).at[low_at].set(2)
    return flat.reshape(N_ROW, N_COL).astype(jnp.int32)


def set_ends(drawn, key, smallest, top_value):
    place = [jax.random.randint(jax.random.fold_in(key, axis), (), 0, length) for axis, length in enumerate(drawn.shape)]
    longest = drawn.shape.index(max(drawn.shape))
    next_to = place[:longest] + [(place[longest] + 1) % drawn.shape[longest]] + place[longest + 1:]
    return drawn.at[tuple(place)].set(smallest).at[tuple(next_to)].set(top_value)


def level_of(stream_key, shape, shards, smallest, largest):
    def one(position, parts):
        heights = jax.random.uniform(jax.random.fold_in(jax.random.fold_in(stream_key, 6), position), (parts,), jnp.float32, smallest / len(shards), largest / len(shards))
        return jnp.repeat(jnp.exp(heights), shape[position] // parts).reshape((-1,) + (1,) * (len(shape) - position - 1))

    loudness = one(*shards[0])
    for cut in shards[1:]:
        loudness = loudness * one(*cut)
    return loudness


def gaussian(key, dims, width, reach, pieces=(), kind=jnp.bfloat16):
    factor_of = level_of(key, dims, pieces, -0.22, 0.18) if pieces else 1.0
    values = jax.random.normal(key, dims, jnp.float32) * width * factor_of
    return jnp.minimum(jnp.maximum(values, -reach), reach).astype(kind)


def setup_inputs(seed: int = 0) -> dict:
    seeds = jax.random.split(jax.random.key(seed), 10)
    return {
        "flexibility": draw_flexibility(jax.random.fold_in(seeds[9], 71), 0),
        "coupling": gaussian(seeds[1], (N_ROW, N_COL, SLOTS, NCOR, IFACE), (IFACE // 16) ** -0.5, 0.75, ((0, 4), (1, 8)), jnp.float32),
        "coarse_inverse": draw_coarse_inverse(jax.random.fold_in(seeds[9], 71), 0),
        "precon_weight": jnp.clip(jnp.exp(math.log(2.0) - 2.0794415 * jax.random.uniform(seeds[3], (N_ROW, N_COL, SLOTS, LINKS, PAIR), jnp.float32) ** level_of(seeds[3], (N_ROW, N_COL, SLOTS, LINKS, PAIR), ((0, 4), (1, 8)), -0.2, 0.2)), 0.25, 2.0),
        "right_side": gaussian(seeds[4], (N_ROW, N_COL, SLOTS, LOADS, LINKS, PAIR), 1.0, 6.0, ((0, 4), (1, 8)), jnp.float32),
        "counts": draw_counts(jax.random.fold_in(seeds[9], 71), 0),
        "partner": jax.vmap(lambda own: jax.random.permutation(own, SLOTS))(jax.random.split(seeds[6], N_ROW * N_COL * LINKS)).reshape((N_ROW, N_COL, LINKS, SLOTS)).astype(jnp.int32),
        "dof_index": jax.vmap(lambda own: jax.random.permutation(own, PAIR))(jax.random.split(seeds[7], N_ROW * N_COL * SLOTS * LINKS)).reshape((N_ROW, N_COL, SLOTS, LINKS, PAIR)).astype(jnp.int32),
        "corner_map": set_ends(jax.random.randint(seeds[8], (N_ROW, N_COL, SLOTS, NCOR), 0, NC), jax.random.fold_in(seeds[8], 1), 0, NC - 1).astype(jnp.int32),
    }


HIGH = lax.Precision.HIGHEST


def link_mask(counts, partner):
    slot_ids = jnp.arange(SLOTS, dtype=jnp.int32)
    live = (slot_ids[None, None, :] < counts[:, :, None]).astype(jnp.float32)
    live_prev = jnp.roll(live, 1, axis=1)
    chosen = (partner[..., None] == slot_ids).astype(jnp.float32)
    link_live = jnp.einsum('rckjp,rcp->rcjk', chosen, live_prev, precision=HIGH)
    return live[..., None] * link_live


def apply_operator(values, flexibility, coupling, coarse_inverse, partner, dof_index, corner_map, mask):
    slot_ids = jnp.arange(SLOTS, dtype=jnp.int32)
    inverse_index = jnp.argsort(dof_index, axis=-1).astype(jnp.int32)
    gather_back = jnp.broadcast_to(inverse_index[:, :, :, None], values.shape)
    forces = jnp.take_along_axis(values, gather_back, axis=5)
    forces_next = jnp.roll(forces, -1, axis=1)
    partner_next = jnp.roll(partner, -1, axis=1)
    chosen_next = (partner_next[..., None] == slot_ids).astype(jnp.float32)
    facing = -jnp.einsum('rckjp,rcjqkw->rcpqkw', chosen_next, forces_next, precision=HIGH)
    shape = values.shape
    force_full = jnp.concatenate([values, facing], axis=4).reshape(shape[0], shape[1], shape[2], shape[3], IFACE)
    answer = jnp.einsum('rcsab,rcsqb->rcsqa', flexibility, force_full, precision=HIGH)
    corner_terms = jnp.einsum('rcsnb,rcsqb->qrcsn', coupling, force_full, precision=HIGH)
    flat_map = corner_map.reshape(-1)
    corner_load = jnp.zeros((LOADS, NC), jnp.float32).at[:, flat_map].add(corner_terms.reshape(LOADS, -1))
    corner_answer = jnp.dot(corner_load, coarse_inverse, precision=HIGH, preferred_element_type=jnp.float32)
    picked = corner_answer[:, flat_map].reshape(LOADS, shape[0], shape[1], shape[2], NCOR)
    answer = answer + jnp.einsum('rcsnb,qrcsn->rcsqb', coupling, picked, precision=HIGH)
    split = answer.reshape(shape[0], shape[1], shape[2], shape[3], 2 * LINKS, PAIR)
    link_part = split[:, :, :, :, :LINKS, :]
    facing_part = jnp.roll(split[:, :, :, :, LINKS:, :], 1, axis=1)
    chosen_own = (partner[..., None] == slot_ids).astype(jnp.float32)
    selected = jnp.einsum('rckjp,rcpqkw->rcjqkw', chosen_own, facing_part, precision=HIGH)
    forward = jnp.broadcast_to(dof_index[:, :, :, None], values.shape)
    selected = jnp.take_along_axis(selected, forward, axis=5)
    return (link_part - selected) * mask


def inner(first, second):
    return jnp.sum(first * second, axis=(0, 1, 2, 4, 5))


def reference(flexibility, coupling, coarse_inverse, precon_weight, right_side, counts, partner, dof_index, corner_map):
    mask = link_mask(counts, partner)[:, :, :, None, :, None]
    weight = precon_weight[:, :, :, None]
    residual = right_side * mask
    solution = jnp.zeros_like(residual)
    precond = weight * residual
    direction = precond
    norm_now = inner(residual, precond)
    for iteration in range(ITERS):
        image = apply_operator(direction, flexibility, coupling, coarse_inverse, partner, dof_index, corner_map, mask)
        alpha = (norm_now / inner(direction, image))[None, None, None, :, None, None]
        solution = solution + alpha * direction
        residual = residual - alpha * image
        precond = weight * residual
        norm_next = inner(residual, precond)
        direction = precond + (norm_next / norm_now)[None, None, None, :, None, None] * direction
        norm_now = norm_next
    return solution, residual
```

```python
import functools
import jax
import jax.numpy as jnp
from jax import lax
from jax.experimental import pallas as pl
from jax.experimental.pallas import tpu as pltpu
from jax.sharding import PartitionSpec as P

ITERS = 3
BOTH = ("row", "col")
LANES = 128


def shifted(x, axis, by):
    devices = lax.axis_size(axis)
    return lax.ppermute(x, axis, [(i, (i + by) % devices) for i in range(devices)])


def swapped(x, bit):
    devices = lax.axis_size(BOTH)
    return lax.ppermute(x, BOTH, [(i, i ^ bit) for i in range(devices)])


def pieces(x, count):
    out = []
    for step in range(count):
        part = x.astype(jnp.bfloat16)
        out.append(part)
        if step + 1 < count:
            x = x - part.astype(jnp.float32)
    return out


def dot_pieces(a, b_parts, a_count=3):
    rows = a.shape[0]
    a_parts = pieces(a, a_count)
    terms = []
    for level, b in enumerate(b_parts):
        used = max(1, a_count - level)
        stacked = jnp.concatenate(a_parts[:used], axis=0) if used > 1 else a_parts[0]
        full = jnp.dot(stacked, b, preferred_element_type=jnp.float32)
        for i in range(used):
            terms.append((i + level, full[i * rows : (i + 1) * rows]))
    terms.sort(key=lambda item: -item[0])
    total = terms[0][1]
    for _, term in terms[1:]:
        total = total + term
    return total


def slot_mask(slots, loads, corners, width):
    row = lax.broadcasted_iota(jnp.int32, (slots * loads, width), 0) // loads
    lane = lax.broadcasted_iota(jnp.int32, (slots * loads, width), 1) // corners
    return row == lane


def to_corners(values, matrix_parts, corners):
    slots, loads, n = values.shape
    full = dot_pieces(values.reshape(slots * loads, n), matrix_parts)
    width = full.shape[1]
    kept = jnp.where(slot_mask(slots, loads, corners, width), full, 0.0)
    return jnp.sum(kept.reshape(slots, loads, width), axis=0)


def from_corners(answer, matrix_parts, slots, corners):
    loads, width = answer.shape
    spread = jnp.broadcast_to(answer[None], (slots, loads, width)).reshape(slots * loads, width)
    spread = jnp.where(slot_mask(slots, loads, corners, width), spread, 0.0)
    out = dot_pieces(spread, matrix_parts)
    return out.reshape(slots, loads, out.shape[1])


def column(x):
    return x[:, :1]


def start_exchange(
    z, partner_ref, inverse_ref, link_t_ref, prev_t_ref, map_ref, parity, corners, coarse_size, send_ref, mine_ref, other_ref
):
    slots, loads, width = z.shape
    links = width // LANES
    for j in range(slots):
        for k in range(links):
            block = z[j, :, k * LANES : (k + 1) * LANES]
            index = jnp.broadcast_to(inverse_ref[j * links + k][None], (loads, LANES))
            send_ref[partner_ref[k, j], :, k * LANES : (k + 1) * LANES] = -jnp.take_along_axis(block, index, axis=1)
    own = to_corners(z, pieces(link_t_ref[...], 3), corners)
    prev = to_corners(send_ref[...], pieces(prev_t_ref[...], 3), corners)
    terms = jnp.concatenate([own, prev], axis=1)
    table = map_ref[...] == lax.broadcasted_iota(jnp.int32, (terms.shape[1], coarse_size), 1)
    load = dot_pieces(terms, [table.astype(jnp.bfloat16)])
    half = coarse_size // 2
    low, high = load[:, :half], load[:, half:]
    mine_ref[...] = jnp.where(parity == 0, low, high)
    other_ref[...] = jnp.where(parity == 0, high, low)


def local_norm(r, z):
    slots, loads, width = r.shape
    return jnp.broadcast_to(jnp.sum(jnp.sum(r * z, axis=0), axis=1, keepdims=True), (loads, LANES))


def first_kernel(
    corners, coarse_size, info_ref, partner_ref, right_ref, weight_ref, dof_ref, link_t_ref, prev_t_ref, map_ref,
    inverse_ref, mask_ref, r_ref, z_ref, norm_ref, send_ref, mine_ref, other_ref,
):
    slots, loads, width = right_ref.shape
    links = width // LANES
    for j in range(slots):
        for k in range(links):
            met = dof_ref[j * links + k : j * links + k + 1, :]
            hit = jnp.broadcast_to(met, (LANES, LANES)) == lax.broadcasted_iota(jnp.int32, (LANES, LANES), 0)
            place = jnp.where(hit, lax.broadcasted_iota(jnp.int32, (LANES, LANES), 1), 0).astype(jnp.float32)
            found = jnp.sum(place.T, axis=0, keepdims=True)
            inverse_ref[j * links + k : j * links + k + 1, :] = found.astype(jnp.int32)
            alive = (j < info_ref[0]) & (partner_ref[k, j] < info_ref[1])
            mask_ref[j : j + 1, k * LANES : (k + 1) * LANES] = jnp.full((1, LANES), jnp.where(alive, 1.0, 0.0), jnp.float32)
    mask = mask_ref[...][:, None, :]
    r = right_ref[...] * mask
    z = weight_ref[...][:, None, :] * r
    r_ref[...] = r
    z_ref[...] = z
    norm_ref[...] = local_norm(r, z)
    start_exchange(
        z, partner_ref, inverse_ref, link_t_ref, prev_t_ref, map_ref, info_ref[2], corners, coarse_size,
        send_ref, mine_ref, other_ref,
    )


def gathered_scalars(blocks_ref, rows):
    total = jnp.sum(blocks_ref[...], axis=0)
    at = 2 * rows
    norm = jnp.concatenate([total[:, at : at + 1], total[:, at + 1 : at + 2]], axis=0)
    product = jnp.concatenate([total[:, at + 2 : at + 3], total[:, at + 3 : at + 4]], axis=0)
    return norm, product


def image_of(
    blocks_ref, rows, partner_ref, own_ref, facing_ref, dof_ref, mask_ref, link_ref, prev_ref, place_ref, corners
):
    slots, loads, width = own_ref.shape
    links = width // LANES
    devices, half, block = blocks_ref.shape
    flat = jnp.concatenate([blocks_ref[e] for e in range(devices)], axis=1)
    turned = jnp.concatenate([pltpu.roll(blocks_ref[e], block - rows, 1) for e in range(devices)], axis=1)
    everything = jnp.concatenate([flat, turned], axis=0)
    table = lax.broadcasted_iota(jnp.int32, (devices * block, place_ref.shape[1]), 0) == place_ref[...]
    picked = dot_pieces(everything, [table.astype(jnp.bfloat16)])
    near = own_ref[...] + from_corners(picked[:, :LANES], pieces(link_ref[...], 3), slots, corners)
    far_ref = from_corners(picked[:, LANES:], pieces(prev_ref[...], 3), slots, corners) + facing_ref[...]
    return near, far_ref


def next_kernel(
    corners, coarse_size, rows, first, last, info_ref, partner_ref, blocks_ref, own_ref, facing_ref, weight_ref, dof_ref,
    inverse_ref, mask_ref, link_ref, prev_ref, link_t_ref, prev_t_ref, map_ref, place_ref, r_ref, z_ref, *refs,
):
    refs = list(refs)
    if not first:
        x_ref, p_ref, s_ref, past_ref = refs[:4]
        refs = refs[4:]
    x_out, r_out = refs[:2]
    far_ref = refs[-1]
    slots, loads, width = own_ref.shape
    links = width // LANES
    norm, product = gathered_scalars(blocks_ref, rows)
    near, far = image_of(
        blocks_ref, rows, partner_ref, own_ref, facing_ref, dof_ref, mask_ref, link_ref, prev_ref, place_ref, corners
    )
    far_ref[...] = far
    jumps = []
    for j in range(slots):
        parts = []
        for k in range(links):
            block = far_ref[partner_ref[k, j], :, k * LANES : (k + 1) * LANES]
            index = jnp.broadcast_to(dof_ref[j * links + k][None], (loads, LANES))
            parts.append(jnp.take_along_axis(block, index, axis=1))
        jumps.append(jnp.concatenate(parts, axis=1)[None])
    mask = mask_ref[...][:, None, :]
    image = (near - jnp.concatenate(jumps, axis=0)) * mask
    if first:
        alpha = norm / product
        p, s = z_ref[...], image
        x = alpha[None] * p
    else:
        ratio = norm / past_ref[:, :1]
        alpha = norm / (product - ratio * norm / past_ref[:, 1:2])
        p = z_ref[...] + ratio[None] * p_ref[...]
        s = image + ratio[None] * s_ref[...]
        x = x_ref[...] + alpha[None] * p
    r = r_ref[...] - alpha[None] * s
    x_out[...] = x
    r_out[...] = r
    if last:
        return
    z_out, p_out, s_out, past_out, norm_out, send_ref, mine_ref, other_ref = refs[2:10]
    z = weight_ref[...][:, None, :] * r
    z_out[...] = z
    p_out[...] = p
    s_out[...] = s
    lane = lax.broadcasted_iota(jnp.int32, past_out.shape, 1)
    past_out[...] = jnp.where(lane == 0, norm, alpha)
    norm_out[...] = local_norm(r, z)
    start_exchange(
        z, partner_ref, inverse_ref, link_t_ref, prev_t_ref, map_ref, info_ref[2], corners, coarse_size,
        send_ref, mine_ref, other_ref,
    )


def flex_near_kernel(values_ref, flex_ref, out_ref):
    out_ref[0] = dot_pieces(values_ref[0], pieces(flex_ref[0], 2))


def flex_far_kernel(values_ref, forces_ref, begun_ref, flex_ref, own_ref, facing_ref, energy_ref):
    width = values_ref.shape[2]
    answer = begun_ref[0] + dot_pieces(forces_ref[0], pieces(flex_ref[0], 2))
    own, facing = answer[:, :width], answer[:, width:]
    own_ref[0] = own
    facing_ref[0] = facing
    work = jnp.sum(values_ref[0] * own + forces_ref[0] * facing, axis=1, keepdims=True)

    @pl.when(pl.program_id(0) == 0)
    def _():
        energy_ref[...] = jnp.zeros_like(energy_ref)

    energy_ref[...] += jnp.broadcast_to(work, energy_ref.shape)


def coarse_kernel(info_ref, mine_ref, other_ref, inverse_ref, energy_ref, norm_ref, out_ref):
    parity = info_ref[2]
    mine, other = mine_ref[...], other_ref[...]
    low, high = jnp.where(parity == 0, mine, other), jnp.where(parity == 0, other, mine)
    load = jnp.concatenate([low, high], axis=1)
    size, rows = inverse_ref.shape
    loads = load.shape[0]
    answer = dot_pieces(load, pieces(inverse_ref[...], 3))
    place = lax.broadcasted_iota(jnp.int32, (size, rows), 0) - info_ref[3] * rows
    chosen = (place == lax.broadcasted_iota(jnp.int32, (size, rows), 1)).astype(jnp.bfloat16)
    own = dot_pieces(load, [chosen])
    product = jnp.sum(answer * own, axis=1, keepdims=True) + energy_ref[:, :1]
    norm = norm_ref[:, :1]
    half = loads // 2
    tail = out_ref.shape[2] - 2 * rows - 4
    block = jnp.concatenate(
        [answer[:half], answer[half:], norm[:half], norm[half:], product[:half], product[half:], jnp.zeros((half, tail), jnp.float32)],
        axis=1,
    )
    out_ref[...] = jnp.broadcast_to(block[None], out_ref.shape)


VMEM = pl.BlockSpec(memory_space=pltpu.VMEM)
SMEM = pl.BlockSpec(memory_space=pltpu.SMEM)
LIMIT = 32 * 1024 * 1024


def shape_of(*dims, dtype=jnp.float32):
    return jax.ShapeDtypeStruct(dims, dtype)


def cost(flops, bytes_accessed):
    return pl.CostEstimate(flops=flops, bytes_accessed=bytes_accessed, transcendentals=0)


def local(
    flexibility,
    coupling,
    coarse_inverse,
    precon_weight,
    right_side,
    counts,
    partner,
    dof_index,
    corner_map,
):
    devices = lax.axis_size(BOTH)
    flex = flexibility[0, 0]
    slots, iface = flex.shape[:2]
    links, width = dof_index.shape[-2:]
    loads = right_side.shape[3]
    corners = corner_map.shape[-1]
    rows, coarse_size = coarse_inverse.shape
    span = links * width
    block = -(-(2 * rows + 4) // LANES) * LANES
    me = lax.axis_index("row") * lax.axis_size("col") + lax.axis_index("col")

    def padded(table):
        return jnp.pad(table.reshape(slots * corners, span), ((0, LANES - slots * corners), (0, 0)))

    own_map = corner_map[0, 0].reshape(1, -1)
    counts_prev = shifted(counts, "col", 1)
    map_prev = shifted(own_map, "col", 1)
    prev = shifted(padded(coupling[0, 0, :, :, span:]), "col", 1)
    link = padded(coupling[0, 0, :, :, :span])
    link_t, prev_t = link.T, prev.T
    pad = jnp.full((1, LANES - slots * corners), -1, jnp.int32)
    maps = jnp.concatenate([own_map, pad, map_prev, pad], axis=1)
    place = jnp.where(maps >= 0, (maps // rows) * block + maps % rows, -1)
    map_column = maps.reshape(-1, 1)
    info = jnp.stack([counts[0, 0], counts_prev[0, 0], lax.axis_index("col") % 2, me]).astype(jnp.int32)
    partners = partner[0, 0]
    dof = dof_index[0, 0].reshape(slots * links, width)
    weight = precon_weight[0, 0].reshape(slots, span)
    right = right_side[0, 0].reshape(slots, loads, span)
    inverse_t = coarse_inverse.T

    state = shape_of(slots, loads, span)
    small = shape_of(loads, LANES)
    half_load = shape_of(loads, coarse_size // 2)
    params = pltpu.CompilerParams(vmem_limit_bytes=LIMIT)

    dof_inverse, mask, r, z, norm, send, mine, other = pl.pallas_call(
        functools.partial(first_kernel, corners, coarse_size),
        out_shape=(shape_of(slots * links, width, dtype=jnp.int32), shape_of(slots, span), state, state, small, state, half_load, half_load),
        in_specs=[SMEM, SMEM] + [VMEM] * 6,
        out_specs=[VMEM] * 8,
        compiler_params=params,
        name="first",
    )(info, partners, right, weight, dof, link_t, prev_t, map_column)

    kept = ()
    for iteration in range(ITERS):
        first, last = iteration == 0, iteration + 1 == ITERS
        forces = shifted(send, "col", -1)
        begun = pl.pallas_call(
            flex_near_kernel,
            grid=(slots,),
            out_shape=shape_of(slots, loads, iface),
            in_specs=[
                pl.BlockSpec((1, loads, span), lambda s: (s, 0, 0)),
                pl.BlockSpec((1, span, iface), lambda s: (s, 0, 0)),
            ],
            out_specs=pl.BlockSpec((1, loads, iface), lambda s: (s, 0, 0)),
            compiler_params=params,
            cost_estimate=cost(2 * slots * loads * span * iface * 6, slots * span * iface * 4),
            name="flex_near",
        )(z, flex)
        total = mine + swapped(other, 1)
        bit = 2
        order = []
        while bit < devices:
            order.append(bit)
            bit *= 2
        columns = lax.axis_size("col")
        order = [b for b in order if b >= columns] + [b for b in order if b < columns]
        for b in order:
            total = total + swapped(total, b)
        rest = swapped(total, 1)
        own, facing, energy = pl.pallas_call(
            flex_far_kernel,
            grid=(slots,),
            out_shape=(state, state, small),
            in_specs=[
                pl.BlockSpec((1, loads, span), lambda s: (s, 0, 0)),
                pl.BlockSpec((1, loads, span), lambda s: (s, 0, 0)),
                pl.BlockSpec((1, loads, iface), lambda s: (s, 0, 0)),
                pl.BlockSpec((1, span, iface), lambda s: (s, 1, 0)),
            ],
            out_specs=[
                pl.BlockSpec((1, loads, span), lambda s: (s, 0, 0)),
                pl.BlockSpec((1, loads, span), lambda s: (s, 0, 0)),
                pl.BlockSpec((loads, LANES), lambda s: (0, 0)),
            ],
            compiler_params=params,
            cost_estimate=cost(2 * slots * loads * span * iface * 6, slots * span * iface * 4),
            name="flex_far",
        )(z, forces, begun, flex)
        facing_prev = shifted(facing, "col", 1)
        blocks = pl.pallas_call(
            coarse_kernel,
            out_shape=shape_of(devices, loads // 2, block),
            in_specs=[SMEM] + [VMEM] * 5,
            out_specs=VMEM,
            compiler_params=params,
            name="coarse",
        )(info, total, rest, inverse_t, energy, norm)
        blocks = lax.all_to_all(blocks, BOTH, 0, 0, tiled=True)
        outs = (state, state)
        if not last:
            outs = outs + (state, state, state, small, small, state, half_load, half_load)
        results = pl.pallas_call(
            functools.partial(next_kernel, corners, coarse_size, rows, first, last),
            out_shape=outs,
            in_specs=[SMEM, SMEM] + [VMEM] * (15 + len(kept)),
            out_specs=[VMEM] * len(outs),
            scratch_shapes=[pltpu.VMEM((slots, loads, span), jnp.float32)],
            compiler_params=params,
            name="step",
        )(
            info, partners, blocks, own, facing_prev, weight, dof, dof_inverse, mask, link, prev, link_t, prev_t,
            map_column, place, r, z, *kept,
        )
        if last:
            x, r = results
        else:
            x, r, z, p, s, past, norm, send, mine, other = results
            kept = (x, p, s, past)
    shape = right_side.shape
    return (x.reshape(shape), r.reshape(shape))


def solution(mesh):
    in_specs = (
        P("row", "col", None, None, None),
        P("row", "col", None, None, None),
        P(("row", "col"), None),
        P("row", "col", None, None, None),
        P("row", "col", None, None, None, None),
        P("row", "col"),
        P("row", "col", None, None),
        P("row", "col", None, None, None),
        P("row", "col", None, None),
    )
    out_specs = (P("row", "col", None, None, None, None), P("row", "col", None, None, None, None))
    return jax.shard_map(local, mesh=mesh, in_specs=in_specs, out_specs=out_specs, check_vma=False)
```

```python
import functools
import jax
import jax.numpy as jnp
from jax import lax
from jax.experimental import pallas as pl
from jax.experimental.pallas import tpu as pltpu
from jax.sharding import PartitionSpec as P

ITERS = 3
BOTH = ("row", "col")
LANES = 128
HALF_TILE = 64


def shifted(x, axis, by):
    devices = lax.axis_size(axis)
    return lax.ppermute(x, axis, [(i, (i + by) % devices) for i in range(devices)])


def swapped(x, bits):
    devices = lax.axis_size(BOTH)
    return lax.ppermute(x, BOTH, [(i, i ^ bits) for i in range(devices)])


def pieces(x, count):
    out = []
    for step in range(count):
        part = x.astype(jnp.bfloat16)
        out.append(part)
        if step + 1 < count:
            x = x - part.astype(jnp.float32)
    return out


def stacked(x, count):
    return jnp.concatenate(pieces(x, count), axis=0)


def matmul(a, b):
    return jnp.dot(a, b, preferred_element_type=jnp.float32)


def through_table(x, table):
    rows = x.shape[0]
    full = matmul(stacked(x, 3), table)
    return full[2 * rows :] + full[rows : 2 * rows] + full[:rows]


def slot_mask(slots, loads, corners):
    row = lax.broadcasted_iota(jnp.int32, (slots * loads, LANES), 0) // loads
    lane = lax.broadcasted_iota(jnp.int32, (slots * loads, LANES), 1) // corners
    return row == lane


def to_corners(values, columns, corners):
    slots, loads, n = values.shape
    rows = slots * loads
    full = matmul(stacked(values.reshape(rows, n), 2), columns)
    full = (full[rows:, :LANES] + full[:rows, LANES:]) + full[:rows, :LANES]
    kept = jnp.where(slot_mask(slots, loads, corners), full, 0.0)
    return jnp.sum(kept.reshape(slots, loads, LANES), axis=0)


def from_corners(answer, matrix, slots, corners):
    loads = answer.shape[0]
    rows = slots * loads
    spread = jnp.broadcast_to(answer[None], (slots, loads, LANES)).reshape(rows, LANES)
    spread = jnp.where(slot_mask(slots, loads, corners), spread, 0.0)
    both = stacked(spread, 2)
    full = matmul(jnp.concatenate([both, both], axis=1), matrix)
    return (full[rows:] + full[:rows]).reshape(slots, loads, full.shape[1])


def corner_rows(coupling, start, width):
    slots, corners, _ = coupling.shape
    parts = [coupling[s, :, start : start + width] for s in range(slots)]
    if slots * corners < LANES:
        parts.append(jnp.zeros((LANES - slots * corners, width), jnp.float32))
    return jnp.concatenate(parts, axis=0)


def prepare_kernel(info_ref, dof_ref, coupling_ref, coarse_ref, inverse_ref, link_ref, link_t_ref, coarse_table_ref):
    slots, links, width = dof_ref.shape[2:]
    span = links * width
    for j in range(slots):
        for k in range(links):
            met = dof_ref[0, 0, j, k : k + 1, :]
            hit = jnp.broadcast_to(met, (width, width)) == lax.broadcasted_iota(jnp.int32, (width, width), 0)
            place = jnp.where(hit, lax.broadcasted_iota(jnp.int32, (width, width), 1), 0).astype(jnp.float32)
            found = jnp.sum(place.T, axis=0, keepdims=True)
            inverse_ref[j * links + k : j * links + k + 1, :] = found.astype(jnp.int32)
    link = corner_rows(coupling_ref[0, 0], 0, span)
    link_ref[...] = stacked(link, 2)
    link_t_ref[...] = jnp.concatenate(pieces(link.T, 2), axis=1)
    rows, size = coarse_ref.shape
    wide = coarse_table_ref.shape[1] // 4
    filled = jnp.concatenate([coarse_ref[...], jnp.zeros((LANES * (-(-wide // LANES)) - rows, size), jnp.float32)], axis=0)
    turned = filled.T[:, :wide]
    place = lax.broadcasted_iota(jnp.int32, (size, wide), 0) - info_ref[0] * rows
    lane = lax.broadcasted_iota(jnp.int32, (size, wide), 1)
    chosen = ((place == lane) & (lane < rows)).astype(jnp.bfloat16)
    coarse_table_ref[...] = jnp.concatenate(pieces(turned, 3) + [chosen], axis=1)


def start_exchange(
    z, partner_ref, inverse_ref, link_t_ref, prev_t_ref, scatter_ref, parity, corners, send_ref, mine_ref, other_ref
):
    slots, loads, span = z.shape
    links = span // LANES
    for j in range(slots):
        for k in range(links):
            block = z[j, :, k * LANES : (k + 1) * LANES]
            index = jnp.broadcast_to(inverse_ref[j * links + k][None], (loads, LANES))
            send_ref[partner_ref[0, 0, k, j], :, k * LANES : (k + 1) * LANES] = -jnp.take_along_axis(block, index, axis=1)
    own = to_corners(z, link_t_ref[...], corners)
    prev = to_corners(send_ref[...], prev_t_ref[...], corners)
    load = through_table(jnp.concatenate([own, prev], axis=1), scatter_ref[...])
    half = load.shape[1] // 2
    low, high = load[:, :half], load[:, half:]
    mine_ref[...] = jnp.where(parity == 0, low, high)
    other_ref[...] = jnp.where(parity == 0, high, low)


def local_norm(r, z):
    slots, loads, span = r.shape
    return jnp.broadcast_to(jnp.sum(jnp.sum(r * z, axis=0), axis=1, keepdims=True), (loads, LANES))


def first_kernel(
    corners, info_ref, partner_ref, counts_ref, prev_info_ref, right_ref, weight_ref, inverse_ref, link_t_ref, prev_coupling_ref,
    map_ref, mask_ref, r_ref, z_ref, norm_ref, send_ref, mine_ref, other_ref, prev_t_ref, scatter_ref,
):
    slots, loads, span = r_ref.shape
    links = span // LANES
    for j in range(slots):
        for k in range(links):
            lanes = slice(k * LANES, (k + 1) * LANES)
            alive = (j < counts_ref[0, 0]) & (partner_ref[0, 0, k, j] < prev_info_ref[0, slots * corners])
            kept = jnp.where(alive, 1.0, 0.0)
            mask_ref[j : j + 1, lanes] = jnp.full((1, LANES), kept, jnp.float32)
            r = right_ref[0, 0, j, :, k, :] * kept
            r_ref[j, :, lanes] = r
            z_ref[j, :, lanes] = weight_ref[0, 0, j, k : k + 1, :] * r
    prev = corner_rows(prev_coupling_ref[...], 0, span)
    prev_t_ref[...] = jnp.concatenate(pieces(prev.T, 2), axis=1)
    scatter_ref[...] = (map_ref[...] == lax.broadcasted_iota(jnp.int32, scatter_ref.shape, 1)).astype(jnp.bfloat16)
    z = z_ref[...]
    norm_ref[...] = local_norm(r_ref[...], z)
    start_exchange(
        z, partner_ref, inverse_ref, link_t_ref, prev_t_ref, scatter_ref, info_ref[1], corners, send_ref, mine_ref, other_ref
    )


def table_kernel(prev_coupling_ref, place_ref, prev_ref, pick_ref):
    prev_ref[...] = stacked(corner_rows(prev_coupling_ref[...], 0, prev_coupling_ref.shape[2]), 2)
    pick_ref[...] = (place_ref[...] == lax.broadcasted_iota(jnp.int32, pick_ref.shape, 0)).astype(jnp.bfloat16)


def gathered_scalars(near_blocks_ref, far_blocks_ref, rows):
    total = jnp.sum(near_blocks_ref[...] + far_blocks_ref[...], axis=0)
    at = 2 * rows
    norm = jnp.concatenate([total[:, at : at + 1], total[:, at + 1 : at + 2]], axis=0)
    product = jnp.concatenate([total[:, at + 2 : at + 3], total[:, at + 3 : at + 4]], axis=0)
    return norm, product


def picked_corners(near_blocks_ref, far_blocks_ref, rows, pick_ref):
    count, half, block = near_blocks_ref.shape
    blocks = [ref[e] for ref in (near_blocks_ref, far_blocks_ref) for e in range(count)]
    low = jnp.concatenate(blocks, axis=1)
    high = jnp.concatenate([pltpu.roll(b, block - rows, 1) for b in blocks], axis=1)
    return through_table(jnp.concatenate([low, high], axis=0), pick_ref[...])


def step_kernel(
    corners, rows, first, last, info_ref, partner_ref, near_blocks_ref, far_blocks_ref, own_ref, facing_ref, weight_ref, dof_ref,
    inverse_ref, mask_ref, link_ref, prev_ref, link_t_ref, prev_t_ref, scatter_ref, pick_ref, r_ref, z_ref, *refs,
):
    refs = list(refs)
    if not first:
        x_ref, p_ref, s_ref, past_ref = refs[:4]
        refs = refs[4:]
    x_out, r_out = refs[:2]
    far_ref = refs[-1]
    slots, loads, span = own_ref.shape
    links = span // LANES
    norm, product = gathered_scalars(near_blocks_ref, far_blocks_ref, rows)
    picked = picked_corners(near_blocks_ref, far_blocks_ref, rows, pick_ref)
    near = own_ref[...] + from_corners(picked[:, :LANES], link_ref[...], slots, corners)
    far_ref[...] = facing_ref[...] + from_corners(picked[:, LANES:], prev_ref[...], slots, corners)
    jumps = []
    for j in range(slots):
        parts = []
        for k in range(links):
            block = far_ref[partner_ref[0, 0, k, j], :, k * LANES : (k + 1) * LANES]
            index = jnp.broadcast_to(dof_ref[0, 0, j, k : k + 1, :], (loads, LANES))
            parts.append(jnp.take_along_axis(block, index, axis=1))
        jumps.append(jnp.concatenate(parts, axis=1)[None])
    image = (near - jnp.concatenate(jumps, axis=0)) * mask_ref[...][:, None, :]
    if first:
        alpha = norm / product
        p, s = z_ref[...], image
        x = alpha[None] * p
    else:
        ratio = norm / past_ref[:, :1]
        alpha = norm / (product - ratio * norm / past_ref[:, 1:2])
        p = z_ref[...] + ratio[None] * p_ref[...]
        s = image + ratio[None] * s_ref[...]
        x = x_ref[...] + alpha[None] * p
    r = r_ref[...] - alpha[None] * s
    if last:
        for j in range(slots):
            for k in range(links):
                x_out[0, 0, j, :, k, :] = x[j, :, k * LANES : (k + 1) * LANES]
                r_out[0, 0, j, :, k, :] = r[j, :, k * LANES : (k + 1) * LANES]
        return
    z_out, p_out, s_out, past_out, norm_out, send_ref, mine_ref, other_ref = refs[2:10]
    x_out[...] = x
    r_out[...] = r
    weight = jnp.concatenate([weight_ref[0, 0, :, k, :] for k in range(links)], axis=1)
    z = weight[:, None, :] * r
    z_out[...] = z
    p_out[...] = p
    s_out[...] = s
    lane = lax.broadcasted_iota(jnp.int32, past_out.shape, 1)
    past_out[...] = jnp.where(lane == 0, norm, alpha)
    norm_out[...] = local_norm(r, z)
    start_exchange(
        z, partner_ref, inverse_ref, link_t_ref, prev_t_ref, scatter_ref, info_ref[1], corners, send_ref, mine_ref, other_ref
    )


def split_kernel(flex_ref, large_ref, small_ref):
    large, small = pieces(flex_ref[0, 0, 0], 2)
    large_ref[0] = large
    small_ref[0] = small


def flex_product(values, large, small):
    loads = values.shape[0]
    full = matmul(stacked(values, 2), large)
    rest = matmul(values.astype(jnp.bfloat16), small)
    return (full[loads:] + rest) + full[:loads]


def flex_near_kernel(values_ref, large_ref, small_ref, out_ref):
    slots, _, width = values_ref.shape
    for s in range(slots):
        out_ref[s] = flex_product(values_ref[s], large_ref[s, :width], small_ref[s, :width])


def flex_far_kernel(values_ref, forces_ref, begun_ref, large_ref, small_ref, own_ref, facing_ref, energy_ref):
    slots, loads, width = values_ref.shape
    work = jnp.zeros((loads, 1), jnp.float32)
    for s in range(slots):
        answer = begun_ref[s] + flex_product(forces_ref[s], large_ref[s, width:], small_ref[s, width:])
        own, facing = answer[:, :width], answer[:, width:]
        own_ref[s] = own
        facing_ref[s] = facing
        work += jnp.sum(values_ref[s] * own + forces_ref[s] * facing, axis=1, keepdims=True)
    energy_ref[...] = jnp.broadcast_to(work, energy_ref.shape)


def coarse_kernel(rows, info_ref, mine_ref, other_ref, table_ref, energy_ref, norm_ref, out_ref):
    parity = info_ref[1]
    mine, other = mine_ref[...], other_ref[...]
    low, high = jnp.where(parity == 0, mine, other), jnp.where(parity == 0, other, mine)
    load = jnp.concatenate([low, high], axis=1)
    loads = load.shape[0]
    wide = table_ref.shape[1] // 4
    full = matmul(stacked(load, 3), table_ref[...])

    def part(i, j):
        return full[i * loads : (i + 1) * loads, j * wide : j * wide + rows]

    answer = ((part(2, 0) + part(1, 1)) + part(0, 2)) + (part(1, 0) + part(0, 1)) + part(0, 0)
    own = (part(2, 3) + part(1, 3)) + part(0, 3)
    product = jnp.sum(answer * own, axis=1, keepdims=True) + energy_ref[:, :1]
    norm = norm_ref[:, :1]
    half = loads // 2
    tail = out_ref.shape[2] - 2 * rows - 4
    out_ref[0] = jnp.concatenate(
        [answer[:half], answer[half:], norm[:half], norm[half:], product[:half], product[half:], jnp.zeros((half, tail), jnp.float32)],
        axis=1,
    )

VMEM = pl.BlockSpec(memory_space=pltpu.VMEM)
SMEM = pl.BlockSpec(memory_space=pltpu.SMEM)
SMALL = pltpu.CompilerParams(vmem_limit_bytes=12 * 1024 * 1024)


def shape_of(*dims, dtype=jnp.float32):
    return pltpu.VMEM(dims, dtype)


def cost(flops, bytes_accessed):
    return pl.CostEstimate(flops=flops, bytes_accessed=bytes_accessed, transcendentals=0)


def gathered(block):
    devices, columns = lax.axis_size(BOTH), lax.axis_size("col")
    for start, stop in ((2, columns), (columns, devices)):
        if stop == 4 * start:
            parts = [block] + [swapped(block, b * start) for b in (1, 2, 3)]
            block = jnp.concatenate(parts, axis=0)
        else:
            while start < stop:
                block = jnp.concatenate([block, swapped(block, start)], axis=0)
                start *= 2
    return block, swapped(block, 1)


def summed(mine, other, between, after):
    devices, columns = lax.axis_size(BOTH), lax.axis_size("col")
    along_rows = [b for b in range(columns, devices, columns)]
    along_columns = [b for b in range(2, columns, 2)]
    total = mine + swapped(other, 1)
    total = between(total)
    for group, hook in ((along_rows, after[0]), (along_columns, after[1])):
        if len(group) <= 3:
            total = sum([swapped(total, b) for b in group], total)
        else:
            for b in [g for g in group if g & (g - 1) == 0]:
                total = total + swapped(total, b)
        total = hook(total)
    return total


def local(
    flexibility,
    coupling,
    coarse_inverse,
    precon_weight,
    right_side,
    counts,
    partner,
    dof_index,
    corner_map,
):
    devices = lax.axis_size(BOTH)
    slots, iface = flexibility.shape[2:4]
    links, width = dof_index.shape[-2:]
    loads = right_side.shape[3]
    corners = corner_map.shape[-1]
    rows, coarse_size = coarse_inverse.shape
    span = links * width
    block = -(-(2 * rows + 4) // LANES) * LANES
    wide = -(-rows // HALF_TILE) * HALF_TILE
    me = lax.axis_index("row") * lax.axis_size("col") + lax.axis_index("col")

    coupling_prev = shifted(coupling[0, 0, :, :, span:], "col", 1)
    spare = jnp.full((1, LANES - slots * corners - 1), -1, jnp.int32)
    own_info = jnp.concatenate([corner_map[0, 0].reshape(1, -1), counts, spare], axis=1)
    prev_info = shifted(own_info, "col", 1)
    unknown = jnp.arange(2 * LANES, dtype=jnp.int32)[None] % LANES < slots * corners
    maps = jnp.where(unknown, jnp.concatenate([own_info, prev_info], axis=1), -1)
    away = jnp.bitwise_xor(maps // rows, me)
    place = jnp.where(unknown, ((away % 2) * (devices // 2) + away // 2) * block + maps % rows, -1)
    map_column = maps.reshape(-1, 1)
    info = jnp.stack([me, lax.axis_index("col") % 2]).astype(jnp.int32)

    state = shape_of(slots, loads, span)
    small = shape_of(loads, LANES)
    half_load = shape_of(loads, coarse_size // 2)
    out_state = jax.ShapeDtypeStruct(right_side.shape, jnp.float32)

    def table(*dims):
        return shape_of(*dims, dtype=jnp.bfloat16)

    inverse, link, link_t, coarse_table = pl.pallas_call(
        prepare_kernel,
        out_shape=(
            shape_of(slots * links, width, dtype=jnp.int32), table(2 * LANES, span), table(span, 2 * LANES),
            table(coarse_size, 4 * wide),
        ),
        in_specs=[SMEM] + [VMEM] * 3,
        out_specs=[VMEM] * 4,
        compiler_params=SMALL,
        name="prepare",
    )(info, dof_index, coupling, coarse_inverse)
    mask, r, z, norm, send, mine, other, prev_t, scatter = pl.pallas_call(
        functools.partial(first_kernel, corners),
        out_shape=(
            shape_of(slots, span), state, state, small, state, half_load, half_load, table(span, 2 * LANES),
            table(2 * LANES, coarse_size),
        ),
        in_specs=[SMEM] * 4 + [VMEM] * 6,
        out_specs=[VMEM] * 9,
        compiler_params=SMALL,
        name="first",
    )(info, partner, counts, prev_info, right_side, precon_weight, inverse, link_t, coupling_prev, map_column)
    prev, pick = pl.pallas_call(
        table_kernel,
        out_shape=(table(2 * LANES, span), table(devices * block, 2 * LANES)),
        in_specs=[VMEM] * 2,
        out_specs=[VMEM] * 2,
        compiler_params=SMALL,
        name="tables",
    )(coupling_prev, place)

    half = pl.BlockSpec((1, span, iface), lambda s, h: (s, h, 0))
    streaming = pltpu.CompilerParams(vmem_limit_bytes=30 * 1024 * 1024)
    large, small_part = pl.pallas_call(
        split_kernel,
        grid=(slots, iface // span),
        out_shape=(table(slots, iface, iface), table(slots, iface, iface)),
        in_specs=[pl.BlockSpec((1, 1, 1, span, iface), lambda s, h: (0, 0, s, h, 0))],
        out_specs=[half, half],
        compiler_params=streaming,
        cost_estimate=cost(0, slots * iface * iface * 8),
        name="split",
    )(flexibility)
    work = cost(2 * slots * loads * span * iface * 6, slots * span * iface * 4)

    def near_call(z):
        return pl.pallas_call(
            flex_near_kernel,
            out_shape=shape_of(slots, loads, iface),
            in_specs=[VMEM] * 3,
            out_specs=VMEM,
            compiler_params=SMALL,
            cost_estimate=work,
            name="flex_near",
        )(z, large, small_part)

    def far_call(z, forces, begun):
        return pl.pallas_call(
            flex_far_kernel,
            out_shape=(state, state, small),
            in_specs=[VMEM] * 5,
            out_specs=[VMEM] * 3,
            compiler_params=SMALL,
            cost_estimate=work,
            name="flex_far",
        )(z, forces, begun, large, small_part)

    kept = ()
    for iteration in range(ITERS):
        first, last = iteration == 0, iteration + 1 == ITERS
        held = {}

        def begin(total):
            total, held["z"] = lax.optimization_barrier((total, z))
            held["begun"] = near_call(held["z"])
            return total

        def after_rows(total):
            total, held["begun"], arrived = lax.optimization_barrier((total, held["begun"], forces))
            held["out"] = far_call(held["z"], arrived, held["begun"])
            return total

        def after_columns(total):
            total, *held["out"] = lax.optimization_barrier((total, *held["out"]))
            return total

        forces = shifted(send, "col", -1)
        total = summed(mine, other, begin, (after_rows, after_columns))
        rest = swapped(total, 1)
        own, facing, energy = held["out"]
        facing_prev = shifted(facing, "col", 1)
        blocks = pl.pallas_call(
            functools.partial(coarse_kernel, rows),
            out_shape=shape_of(1, loads // 2, block),
            in_specs=[SMEM] + [VMEM] * 5,
            out_specs=VMEM,
            compiler_params=SMALL,
            name="coarse",
        )(info, total, rest, coarse_table, energy, norm)
        near_blocks, far_blocks = gathered(blocks)
        outs = (out_state, out_state) if last else (state,) * 5 + (small, small, state, half_load, half_load)
        results = pl.pallas_call(
            functools.partial(step_kernel, corners, rows, first, last),
            out_shape=outs,
            in_specs=[SMEM, SMEM] + [VMEM] * (16 + len(kept)),
            out_specs=[VMEM] * len(outs),
            scratch_shapes=[pltpu.VMEM((slots, loads, span), jnp.float32)],
            compiler_params=SMALL,
            name="step",
        )(
            info, partner, near_blocks, far_blocks, own, facing_prev, precon_weight, dof_index, inverse, mask, link, prev, link_t, prev_t,
            scatter, pick, r, z, *kept,
        )
        if last:
            return results
        x, r, z, p, s, past, norm, send, mine, other = results
        kept = (x, p, s, past)


def solution(mesh):
    in_specs = (
        P("row", "col", None, None, None),
        P("row", "col", None, None, None),
        P(("row", "col"), None),
        P("row", "col", None, None, None),
        P("row", "col", None, None, None, None),
        P("row", "col"),
        P("row", "col", None, None),
        P("row", "col", None, None, None),
        P("row", "col", None, None),
    )
    out_specs = (P("row", "col", None, None, None, None), P("row", "col", None, None, None, None))
    return jax.shard_map(local, mesh=mesh, in_specs=in_specs, out_specs=out_specs, check_vma=False)
```

```python
import functools
import jax
import jax.numpy as jnp
from jax import lax
from jax.experimental import pallas as pl
from jax.experimental.pallas import tpu as pltpu
from jax.sharding import PartitionSpec as P

ITERS = 3
BOTH = ("row", "col")
LANES = 128
BUFFERS = 6


def shifted(x, axis, by):
    devices = lax.axis_size(axis)
    return lax.ppermute(x, axis, [(i, (i + by) % devices) for i in range(devices)])


def swapped(x, bits):
    devices = lax.axis_size(BOTH)
    return lax.ppermute(x, BOTH, [(i, i ^ bits) for i in range(devices)])


def pieces(x, count):
    out = []
    for step in range(count):
        part = x.astype(jnp.bfloat16)
        out.append(part)
        if step + 1 < count:
            x = x - part.astype(jnp.float32)
    return out


def stacked(x, count):
    return jnp.concatenate(pieces(x, count), axis=0)


def matmul(a, b):
    return jnp.dot(a, b, preferred_element_type=jnp.float32)


def through_table(x, table):
    rows = x.shape[0]
    full = matmul(stacked(x, 3), table)
    return full[2 * rows :] + full[rows : 2 * rows] + full[:rows]


def slot_mask(slots, loads, corners):
    row = lax.broadcasted_iota(jnp.int32, (slots * loads, LANES), 0) // loads
    lane = lax.broadcasted_iota(jnp.int32, (slots * loads, LANES), 1) // corners
    return row == lane


def to_corners(values, columns, corners):
    slots, loads, n = values.shape
    rows = slots * loads
    full = matmul(stacked(values.reshape(rows, n), 2), columns)
    full = (full[rows:, :LANES] + full[:rows, LANES:]) + full[:rows, :LANES]
    kept = jnp.where(slot_mask(slots, loads, corners), full, 0.0)
    return jnp.sum(kept.reshape(slots, loads, LANES), axis=0)


def from_corners(answer, matrix, slots, corners):
    loads = answer.shape[0]
    rows = slots * loads
    spread = jnp.broadcast_to(answer[None], (slots, loads, LANES)).reshape(rows, LANES)
    spread = jnp.where(slot_mask(slots, loads, corners), spread, 0.0)
    both = stacked(spread, 2)
    full = matmul(jnp.concatenate([both, both], axis=1), matrix)
    return (full[rows:] + full[:rows]).reshape(slots, loads, full.shape[1])


def corner_rows(coupling, width):
    slots, corners, _ = coupling.shape
    parts = [coupling[s, :, :width] for s in range(slots)]
    if slots * corners < LANES:
        parts.append(jnp.zeros((LANES - slots * corners, width), jnp.float32))
    return jnp.concatenate(parts, axis=0)


def split_in_turn(flex_ref, part, large_ref, small_ref, buffer, sem):
    slots, iface = flex_ref.shape[2:4]
    depth = buffer.shape[1]
    per_slot = iface // 2 // depth
    chunks = slots * per_slot

    def chunk(c):
        first = pl.multiple_of(part * (iface // 2) + (c % per_slot) * depth, depth)
        return pltpu.make_async_copy(
            flex_ref.at[0, 0, c // per_slot, pl.ds(first, depth), :], buffer.at[c % BUFFERS], sem.at[c % BUFFERS]
        )

    def begin():
        for c in range(min(BUFFERS, chunks)):
            chunk(c).start()

    def one(c, carry):
        chunk(c).wait()
        rows = pl.ds(pl.multiple_of((c % per_slot) * depth, depth), depth)
        large, small = pieces(buffer[c % BUFFERS], 2)
        large_ref[c // per_slot, rows, :] = large
        small_ref[c // per_slot, rows, :] = small

        @pl.when(c + BUFFERS < chunks)
        def _():
            chunk(c + BUFFERS).start()

        return carry

    return begin, lambda: lax.fori_loop(0, chunks, one, 0)


def split_kernel(flex_ref, large_ref, small_ref, buffer, sem):
    begin, end = split_in_turn(flex_ref, 1, large_ref, small_ref, buffer, sem)
    begin()
    end()


def pack_kernel(coupling_ref, map_ref, counts_ref, out_ref, sem):
    slots, corners = map_ref.shape[2:]
    span = out_ref.shape[2] - LANES
    copy = pltpu.make_async_copy(coupling_ref.at[0, 0, :, :, pl.ds(span, span)], out_ref.at[:, :, pl.ds(0, span)], sem)
    copy.start()
    padded = jnp.concatenate([map_ref[0, 0].astype(jnp.float32), jnp.zeros((8 - slots, corners), jnp.float32)], axis=0)
    column = jnp.concatenate([padded, jnp.zeros((8, LANES - corners), jnp.float32)], axis=1).T
    lane = lax.broadcasted_iota(jnp.int32, (corners, LANES), 1)
    live = jnp.full((corners, LANES), counts_ref[0, 0], jnp.int32).astype(jnp.float32)
    for s in range(slots):
        out_ref[s, :, span:] = jnp.where(lane == 0, column[:corners, s : s + 1], live)
    copy.wait()


def prepare_kernel(
    info_ref, flex_ref, coupling_ref, dof_ref, right_ref, weight_ref, large_ref, small_ref, inverse_ref, dof_rows_ref, link_ref,
    link_t_ref, right_rows_ref, weight_rows_ref, buffer, coupling_buffer, dof_buffer, right_buffer, weight_buffer, flex_sem, sem,
):
    slots, links, width = dof_buffer.shape
    span = links * width
    begin, end = split_in_turn(flex_ref, 0, large_ref, small_ref, buffer, flex_sem)
    others = [
        pltpu.make_async_copy(dof_ref.at[0, 0], dof_buffer, sem.at[0]),
        pltpu.make_async_copy(coupling_ref.at[0, 0], coupling_buffer, sem.at[1]),
        pltpu.make_async_copy(right_ref.at[0, 0], right_buffer, sem.at[2]),
        pltpu.make_async_copy(weight_ref.at[0, 0], weight_buffer, sem.at[3]),
    ]
    for copy in others:
        copy.start()
    begin()
    others[0].wait()
    for j in range(slots):
        for k in range(links):
            at = slice(j * links + k, j * links + k + 1)
            met = dof_buffer[j, k : k + 1, :]
            hit = jnp.broadcast_to(met, (width, width)) == lax.broadcasted_iota(jnp.int32, (width, width), 0)
            place = jnp.where(hit, lax.broadcasted_iota(jnp.int32, (width, width), 1), 0).astype(jnp.float32)
            found = jnp.sum(place.T, axis=0, keepdims=True)
            inverse_ref[at, :] = found.astype(jnp.int32)
            dof_rows_ref[at, :] = met
    others[1].wait()
    link = corner_rows(coupling_buffer[...], span)
    link_ref[...] = stacked(link, 2)
    link_t_ref[...] = jnp.concatenate(pieces(link.T, 2), axis=1)
    others[2].wait()
    others[3].wait()
    for j in range(slots):
        for k in range(links):
            lanes = slice(k * width, (k + 1) * width)
            right_rows_ref[j, :, lanes] = right_buffer[j, :, k, :]
            weight_rows_ref[j : j + 1, lanes] = weight_buffer[j, k : k + 1, :]
    end()


def start_exchange(
    z, norm, partner_ref, inverse_ref, link_t_ref, prev_t_ref, scatter_ref, parity, corners, send_ref, mine_ref, other_ref
):
    slots, loads, span = z.shape
    links = span // LANES
    for j in range(slots):
        for k in range(links):
            block = z[j, :, k * LANES : (k + 1) * LANES]
            index = jnp.broadcast_to(inverse_ref[j * links + k][None], (loads, LANES))
            send_ref[partner_ref[0, 0, k, j], :, k * LANES : (k + 1) * LANES] = -jnp.take_along_axis(block, index, axis=1)
    own = to_corners(z, link_t_ref[...], corners)
    prev = to_corners(send_ref[...], prev_t_ref[...], corners)
    load = through_table(jnp.concatenate([own, prev], axis=1), scatter_ref[...])
    half = load.shape[1] // 2
    low, high = load[:, :half], load[:, half:]
    mine_ref[:, :half] = jnp.where(parity == 0, low, high)
    other_ref[:, :half] = jnp.where(parity == 0, high, low)
    spare = jnp.where(lax.broadcasted_iota(jnp.int32, (loads, LANES), 1) == 0, norm, 0.0)
    mine_ref[:, half:] = spare
    other_ref[:, half:] = spare


def local_norm(r, z):
    return jnp.sum(jnp.sum(r * z, axis=0), axis=1, keepdims=True)


def first_kernel(
    corners, info_ref, partner_ref, counts_ref, right_ref, weight_ref, inverse_ref, link_t_ref, map_ref, prev_coupling_ref,
    mask_ref, r_ref, z_ref, send_ref, mine_ref, other_ref, prev_t_ref, scatter_ref,
):
    slots, loads, span = r_ref.shape
    links = span // LANES
    live_prev = prev_coupling_ref[0, 0:1, span:][:, 1:2]
    for j in range(slots):
        live = jnp.where(j < counts_ref[0, 0], live_prev, 0.0)
        for k in range(links):
            met = jnp.full((1, LANES), partner_ref[0, 0, k, j], jnp.int32).astype(jnp.float32)
            mask_ref[j : j + 1, k * LANES : (k + 1) * LANES] = jnp.where(met < live, 1.0, 0.0)
    r = right_ref[...] * mask_ref[...][:, None, :]
    z = weight_ref[...][:, None, :] * r
    r_ref[...] = r
    z_ref[...] = z
    prev_t_ref[...] = jnp.concatenate(pieces(corner_rows(prev_coupling_ref[...], span).T, 2), axis=1)
    size = scatter_ref.shape[1]
    lane = lax.broadcasted_iota(jnp.int32, (corners, size), 1)
    padded = jnp.concatenate([map_ref[0, 0].astype(jnp.float32), jnp.zeros((8 - slots, corners), jnp.float32)], axis=0)
    column = jnp.concatenate([padded, jnp.zeros((8, LANES - corners), jnp.float32)], axis=1).T
    own = [column[:corners, s : s + 1] for s in range(slots)]
    prev = [prev_coupling_ref[s, :, span:][:, :1] for s in range(slots)]
    for side, columns in enumerate((own, prev)):
        parts = [(c.astype(jnp.int32) == lane).astype(jnp.float32) for c in columns]
        if slots * corners < LANES:
            parts.append(jnp.zeros((LANES - slots * corners, size), jnp.float32))
        scatter_ref[side * LANES : (side + 1) * LANES, :] = jnp.concatenate(parts, axis=0).astype(jnp.bfloat16)
    start_exchange(
        z, local_norm(r, z), partner_ref, inverse_ref, link_t_ref, prev_t_ref, scatter_ref, info_ref[0], corners,
        send_ref, mine_ref, other_ref,
    )


def table_kernel(rows, levels, info_ref, prev_coupling_ref, map_ref, *refs):
    *parts, prev_ref, pick_ref, coarse_ref, joined_ref = refs
    span = prev_ref.shape[1]
    prev_ref[...] = stacked(corner_rows(prev_coupling_ref[...], span), 2)
    slots, corners = map_ref.shape[2:]
    side_rows = len(parts) // 2
    per_level = rows * len(parts)
    lines = []
    own = [map_ref[0, 0, s : s + 1, :] for s in range(slots)]
    filled = jnp.zeros((LANES - corners, LANES), jnp.float32)
    prev = [jnp.concatenate([prev_coupling_ref[s, :, span:], filled], axis=0).T for s in range(slots)]
    prev = [turned[:1, :corners].astype(jnp.int32) for turned in prev]
    for line in (own, prev):
        if slots * corners < LANES:
            line.append(jnp.full((1, LANES - slots * corners), -1, jnp.int32))
        lines += line
    maps = jnp.concatenate(lines, axis=1)
    row = maps // (2 * rows * levels)
    rest = maps - row * (2 * rows * levels)
    level = rest // (2 * rows)
    within = rest - level * (2 * rows)
    place = jnp.bitwise_xor(level, info_ref[2]) * per_level + row * (2 * rows) + within
    place = jnp.where(maps >= 0, place, -1)
    pick_ref[...] = (place == lax.broadcasted_iota(jnp.int32, pick_ref.shape, 0)).astype(jnp.bfloat16)
    for core in range(2):
        for away in range(side_rows):
            at = jnp.bitwise_xor(info_ref[1], away) * (2 * rows) + jnp.bitwise_xor(info_ref[0], core) * rows
            joined_ref[pl.ds(pl.multiple_of(at, 8), rows), :] = parts[core * side_rows + away][...]
    coarse_ref[...] = jnp.concatenate(pieces(joined_ref[...].T, 2), axis=1)


def step_kernel(
    corners, levels, first, last, info_ref, partner_ref, own_ref, facing_ref, weight_ref, dof_ref,
    inverse_ref, mask_ref, link_ref, prev_ref, link_t_ref, prev_t_ref, scatter_ref, pick_ref, r_ref, z_ref, *refs,
):
    refs = list(refs)
    block_refs = refs[:levels]
    refs = refs[levels:]
    if not first:
        x_ref, p_ref, s_ref, past_ref = refs[:4]
        refs = refs[4:]
    x_out, r_out = refs[:2]
    far_ref = refs[-1]
    slots, loads, span = own_ref.shape
    links = span // LANES
    per_level = pick_ref.shape[0] // levels
    spare = block_refs[0][:, per_level:]
    norm = spare[:, 1:2]
    product = spare[:, :1]
    for ref in block_refs[1:]:
        product = product + ref[:, per_level:][:, :1]
    gathered = jnp.concatenate([ref[:, :per_level] for ref in block_refs], axis=1)
    picked = through_table(gathered, pick_ref[...])
    near = own_ref[...] + from_corners(picked[:, :LANES], link_ref[...], slots, corners)
    far_ref[...] = facing_ref[...] + from_corners(picked[:, LANES:], prev_ref[...], slots, corners)
    jumps = []
    for j in range(slots):
        parts = []
        for k in range(links):
            block = far_ref[partner_ref[0, 0, k, j], :, k * LANES : (k + 1) * LANES]
            index = jnp.broadcast_to(dof_ref[j * links + k][None], (loads, LANES))
            parts.append(jnp.take_along_axis(block, index, axis=1))
        jumps.append(jnp.concatenate(parts, axis=1)[None])
    image = (near - jnp.concatenate(jumps, axis=0)) * mask_ref[...][:, None, :]
    if first:
        alpha = norm / product
        p, s = z_ref[...], image
        x = alpha[None] * p
    else:
        ratio = norm / past_ref[:, :1]
        alpha = norm / (product - ratio * norm / past_ref[:, 1:2])
        p = z_ref[...] + ratio[None] * p_ref[...]
        s = image + ratio[None] * s_ref[...]
        x = x_ref[...] + alpha[None] * p
    r = r_ref[...] - alpha[None] * s
    if last:
        for j in range(slots):
            for k in range(links):
                x_out[0, 0, j, :, k, :] = x[j, :, k * LANES : (k + 1) * LANES]
                r_out[0, 0, j, :, k, :] = r[j, :, k * LANES : (k + 1) * LANES]
        return
    z_out, p_out, s_out, past_out, send_ref, mine_ref, other_ref = refs[2:9]
    x_out[...] = x
    r_out[...] = r
    z = weight_ref[...][:, None, :] * r
    z_out[...] = z
    p_out[...] = p
    s_out[...] = s
    lane = lax.broadcasted_iota(jnp.int32, past_out.shape, 1)
    past_out[...] = jnp.where(lane == 0, norm, alpha)
    start_exchange(
        z, local_norm(r, z), partner_ref, inverse_ref, link_t_ref, prev_t_ref, scatter_ref, info_ref[0], corners,
        send_ref, mine_ref, other_ref,
    )


def flex_product(values, large, small):
    loads = values.shape[0]
    full = matmul(stacked(values, 2), large)
    rest = matmul(values.astype(jnp.bfloat16), small)
    return (full[loads:] + rest) + full[:loads]


def flex_near_kernel(values_ref, large_ref, small_ref, out_ref):
    slots, _, width = values_ref.shape
    for s in range(slots):
        out_ref[s] = flex_product(values_ref[s], large_ref[s], small_ref[s])


def flex_far_kernel(values_ref, forces_ref, begun_ref, large_ref, small_ref, own_ref, facing_ref, energy_ref):
    slots, loads, width = values_ref.shape
    work = jnp.zeros((loads, 1), jnp.float32)
    for s in range(slots):
        answer = begun_ref[s] + flex_product(forces_ref[s], large_ref[s], small_ref[s])
        own, facing = answer[:, :width], answer[:, width:]
        own_ref[s] = own
        facing_ref[s] = facing
        work += jnp.sum(values_ref[s] * own + forces_ref[s] * facing, axis=1, keepdims=True)
    half = energy_ref.shape[1] - LANES
    energy_ref[:, :half] = jnp.zeros((loads, half), jnp.float32)
    energy_ref[:, half:] = jnp.where(lax.broadcasted_iota(jnp.int32, (loads, LANES), 1) == 1, work, 0.0)


def coarse_kernel(rows, levels, info_ref, mine_ref, other_ref, table_ref, out_ref):
    parity = info_ref[0]
    half = mine_ref.shape[1] - LANES
    mine, other = mine_ref[:, :half], other_ref[:, :half]
    low, high = jnp.where(parity == 0, mine, other), jnp.where(parity == 0, other, mine)
    load = jnp.concatenate([low, high], axis=1)
    loads, size = load.shape
    per_level = table_ref.shape[1] // 2
    full = matmul(stacked(load, 3), table_ref[...])

    def part(i, j):
        return full[i * loads : (i + 1) * loads, j * per_level : (j + 1) * per_level]

    answer = ((part(2, 0) + part(1, 1)) + (part(1, 0) + part(0, 1))) + part(0, 0)
    stretch = 2 * rows
    own = jnp.zeros((loads, per_level), jnp.float32)
    for level in range(levels):
        starts = range(level * stretch, size, levels * stretch)
        own = jnp.where(info_ref[2] == level, jnp.concatenate([load[:, a : a + stretch] for a in starts], axis=1), own)
    mine_spare, other_spare = mine_ref[:, half:], other_ref[:, half:]
    product = jnp.sum(answer * own, axis=1, keepdims=True) + (mine_spare[:, 1:2] + other_spare[:, 1:2])
    lane = lax.broadcasted_iota(jnp.int32, (loads, LANES), 1)
    out_ref[:, :per_level] = answer
    out_ref[:, per_level:] = jnp.where(lane == 0, product, jnp.where(lane == 1, mine_spare[:, :1], 0.0))


VMEM = pl.BlockSpec(memory_space=pltpu.VMEM)
SMEM = pl.BlockSpec(memory_space=pltpu.SMEM)
HBM = pl.BlockSpec(memory_space=pltpu.HBM)
LITTLE = pl.CostEstimate(flops=1024, bytes_accessed=1024, transcendentals=0)
PARAMS = pltpu.CompilerParams(vmem_limit_bytes=14 * 1024 * 1024)


def shape_of(*dims, dtype=jnp.float32):
    return pltpu.VMEM(dims, dtype)


def gathered_along(blocks, bits):
    if len(bits) == 2 and len(blocks) == 1:
        return blocks + [swapped(blocks[0], b) for b in (bits[0], bits[1], bits[0] + bits[1])]
    for bit in bits:
        blocks = blocks + [swapped(b, bit) for b in blocks]
    return blocks


def summed_along(total, bits):
    if len(bits) == 2:
        return sum([swapped(total, b) for b in (bits[0], bits[1], bits[0] + bits[1])], total)
    for bit in bits:
        total = total + swapped(total, bit)
    return total


def powers(start, stop):
    out = []
    while start < stop:
        out.append(start)
        start *= 2
    return out


def local(
    flexibility,
    coupling,
    coarse_inverse,
    precon_weight,
    right_side,
    counts,
    partner,
    dof_index,
    corner_map,
):
    devices, columns = lax.axis_size(BOTH), lax.axis_size("col")
    levels = columns // 2
    slots, iface = flexibility.shape[2:4]
    links, width = dof_index.shape[-2:]
    loads = right_side.shape[3]
    corners = corner_map.shape[-1]
    rows, coarse_size = coarse_inverse.shape
    span = links * width
    per_level = coarse_size // levels
    row_bits, level_bits = powers(columns, devices), powers(2, columns)
    at_col = lax.axis_index("col")
    info = jnp.stack([at_col % 2, lax.axis_index("row"), at_col // 2]).astype(jnp.int32)

    coupling = pltpu.with_memory_space_constraint(coupling, pltpu.HBM)
    to_next = pl.pallas_call(
        pack_kernel,
        out_shape=shape_of(slots, corners, span + LANES),
        in_specs=[HBM, VMEM, SMEM],
        out_specs=VMEM,
        scratch_shapes=[pltpu.SemaphoreType.DMA],
        compiler_params=PARAMS,
        cost_estimate=LITTLE,
        name="pack",
    )(coupling, corner_map, counts)
    prev_coupling = shifted(to_next, "col", 1)
    coarse_parts = gathered_along([coarse_inverse], row_bits)
    coarse_parts = coarse_parts + [swapped(part, 1) for part in coarse_parts]

    state = shape_of(slots, loads, span)
    small = shape_of(loads, LANES)
    half_load = shape_of(loads, coarse_size // 2 + LANES)
    out_state = jax.ShapeDtypeStruct(right_side.shape, jnp.float32)

    def table(*dims):
        return shape_of(*dims, dtype=jnp.bfloat16)

    depth = iface // 4
    half_pieces = (table(slots, span, iface), table(slots, span, iface))
    buffers = [pltpu.VMEM((BUFFERS, depth, iface), jnp.float32)]
    flex = pltpu.with_memory_space_constraint(flexibility, pltpu.HBM)
    in_place = [pltpu.with_memory_space_constraint(a, pltpu.HBM) for a in (dof_index, right_side, precon_weight)]
    near_large, near_small, inverse, dof, link, link_t, right, weight = pl.pallas_call(
        prepare_kernel,
        out_shape=half_pieces
        + (
            shape_of(slots * links, width, dtype=jnp.int32), shape_of(slots * links, width, dtype=jnp.int32),
            table(2 * LANES, span), table(span, 2 * LANES), state, shape_of(slots, span),
        ),
        in_specs=[SMEM] + [HBM] * 5,
        out_specs=[VMEM] * 8,
        scratch_shapes=buffers
        + [
            pltpu.VMEM(coupling.shape[2:], jnp.float32),
            pltpu.VMEM((slots, links, width), jnp.int32),
            pltpu.VMEM(right_side.shape[2:], jnp.float32),
            pltpu.VMEM((slots, links, width), jnp.float32),
            pltpu.SemaphoreType.DMA((BUFFERS,)),
            pltpu.SemaphoreType.DMA((4,)),
        ],
        compiler_params=PARAMS,
        cost_estimate=LITTLE,
        name="prepare",
    )(info, flex, coupling, *in_place)
    mask, r, z, send, mine, other, prev_t, scatter = pl.pallas_call(
        functools.partial(first_kernel, corners),
        out_shape=(
            shape_of(slots, span), state, state, state, half_load, half_load, table(span, 2 * LANES),
            table(2 * LANES, coarse_size),
        ),
        in_specs=[SMEM] * 3 + [VMEM] * 6,
        out_specs=[VMEM] * 8,
        compiler_params=PARAMS,
        cost_estimate=LITTLE,
        name="first",
    )(info, partner, counts, right, weight, inverse, link_t, corner_map, prev_coupling)

    def split_far(flex):
        return pl.pallas_call(
            split_kernel,
            out_shape=half_pieces,
            in_specs=[HBM],
            out_specs=[VMEM] * 2,
            scratch_shapes=buffers + [pltpu.SemaphoreType.DMA((BUFFERS,))],
            compiler_params=PARAMS,
            cost_estimate=LITTLE,
            name="split",
        )(pltpu.with_memory_space_constraint(flex, pltpu.HBM))

    def tables():
        return pl.pallas_call(
            functools.partial(table_kernel, rows, levels),
            out_shape=(table(2 * LANES, span), table(coarse_size, 2 * LANES), table(coarse_size, 2 * per_level)),
            in_specs=[SMEM] + [VMEM] * (2 + len(coarse_parts)),
            out_specs=[VMEM] * 3,
            scratch_shapes=[pltpu.VMEM((per_level, coarse_size), jnp.float32)],
            compiler_params=pltpu.CompilerParams(vmem_limit_bytes=max(14 * 1024 * 1024, 16 * per_level * coarse_size)),
            cost_estimate=LITTLE,
            name="tables",
        )(info, prev_coupling, corner_map, *coarse_parts)

    kept = ()
    for iteration in range(ITERS):
        first, last = iteration == 0, iteration + 1 == ITERS
        forces = shifted(send, "col", -1)
        total = mine + swapped(other, 1)
        total, held, flexibility = lax.optimization_barrier((total, z, flexibility))
        if first:
            far_large, far_small = split_far(flexibility)
        begun = pl.pallas_call(
            flex_near_kernel,
            out_shape=shape_of(slots, loads, iface),
            in_specs=[VMEM] * 3,
            out_specs=VMEM,
            compiler_params=PARAMS,
            cost_estimate=LITTLE,
            name="flex_near",
        )(held, near_large, near_small)
        total = summed_along(total, level_bits)
        own, facing, energy = pl.pallas_call(
            flex_far_kernel,
            out_shape=(state, state, half_load),
            in_specs=[VMEM] * 5,
            out_specs=[VMEM] * 3,
            compiler_params=PARAMS,
            cost_estimate=LITTLE,
            name="flex_far",
        )(held, forces, begun, far_large, far_small)
        total = summed_along(total + energy, row_bits)
        rest = swapped(total, 1)
        facing_prev = shifted(facing, "col", 1)
        if first:
            prev, pick, coarse_table = tables()
        block = pl.pallas_call(
            functools.partial(coarse_kernel, rows, levels),
            out_shape=shape_of(loads, per_level + LANES),
            in_specs=[SMEM] + [VMEM] * 3,
            out_specs=VMEM,
            compiler_params=PARAMS,
            cost_estimate=LITTLE,
            name="coarse",
        )(info, total, rest, coarse_table)
        blocks = gathered_along([block], level_bits)
        outs = (out_state, out_state) if last else (state,) * 5 + (small, state, half_load, half_load)
        results = pl.pallas_call(
            functools.partial(step_kernel, corners, levels, first, last),
            out_shape=outs,
            in_specs=[SMEM, SMEM] + [VMEM] * (14 + levels + len(kept)),
            out_specs=[VMEM] * len(outs),
            scratch_shapes=[pltpu.VMEM((slots, loads, span), jnp.float32)],
            compiler_params=PARAMS,
            cost_estimate=LITTLE,
            name="step",
        )(
            info, partner, own, facing_prev, weight, dof, inverse, mask, link, prev, link_t, prev_t,
            scatter, pick, r, z, *blocks, *kept,
        )
        if last:
            return results
        x, r, z, p, s, past, send, mine, other = results
        kept = (x, p, s, past)


def solution(mesh):
    in_specs = (
        P("row", "col", None, None, None),
        P("row", "col", None, None, None),
        P(("row", "col"), None),
        P("row", "col", None, None, None),
        P("row", "col", None, None, None, None),
        P("row", "col"),
        P("row", "col", None, None),
        P("row", "col", None, None, None),
        P("row", "col", None, None),
    )
    out_specs = (P("row", "col", None, None, None, None), P("row", "col", None, None, None, None))
    return jax.shard_map(local, mesh=mesh, in_specs=in_specs, out_specs=out_specs, check_vma=False)
```

```python
import functools
import jax
import jax.numpy as jnp
from jax import lax
from jax.experimental import pallas as pl
from jax.experimental.pallas import tpu as pltpu
from jax.sharding import PartitionSpec as P

ITERS = 3
BOTH = ("row", "col")
LANES = 128
BUFFERS = 6


def shifted(x, axis, by):
    devices = lax.axis_size(axis)
    return lax.ppermute(x, axis, [(i, (i + by) % devices) for i in range(devices)])


def swapped(x, bits):
    devices = lax.axis_size(BOTH)
    return lax.ppermute(x, BOTH, [(i, i ^ bits) for i in range(devices)])


def pieces(x, count):
    out = []
    for step in range(count):
        part = x.astype(jnp.bfloat16)
        out.append(part)
        if step + 1 < count:
            x = x - part.astype(jnp.float32)
    return out


def stacked(x, count):
    return jnp.concatenate(pieces(x, count), axis=0)


def matmul(a, b):
    return jnp.dot(a, b, preferred_element_type=jnp.float32)


def through_table(x, table):
    rows = x.shape[0]
    full = matmul(stacked(x, 3), table)
    return full[2 * rows :] + full[rows : 2 * rows] + full[:rows]


def slot_mask(slots, loads, corners):
    row = lax.broadcasted_iota(jnp.int32, (slots * loads, LANES), 0) // loads
    lane = lax.broadcasted_iota(jnp.int32, (slots * loads, LANES), 1) // corners
    return row == lane


def to_corners(values, columns, corners):
    slots, loads, n = values.shape
    rows = slots * loads
    full = matmul(stacked(values.reshape(rows, n), 2), columns)
    full = (full[rows:, :LANES] + full[:rows, LANES:]) + full[:rows, :LANES]
    kept = jnp.where(slot_mask(slots, loads, corners), full, 0.0)
    return jnp.sum(kept.reshape(slots, loads, LANES), axis=0)


def from_corners(answer, matrix, slots, corners):
    loads = answer.shape[0]
    rows = slots * loads
    spread = jnp.broadcast_to(answer[None], (slots, loads, LANES)).reshape(rows, LANES)
    spread = jnp.where(slot_mask(slots, loads, corners), spread, 0.0)
    both = stacked(spread, 2)
    full = matmul(jnp.concatenate([both, both], axis=1), matrix)
    return (full[rows:] + full[:rows]).reshape(slots, loads, full.shape[1])


def corner_rows(coupling, width):
    slots, corners, _ = coupling.shape
    parts = [coupling[s, :, :width] for s in range(slots)]
    if slots * corners < LANES:
        parts.append(jnp.zeros((LANES - slots * corners, width), jnp.float32))
    return jnp.concatenate(parts, axis=0)


def split_in_turn(flex_ref, part, large_ref, small_ref, buffer, sem):
    slots, iface = flex_ref.shape[2:4]
    depth = buffer.shape[1]
    per_slot = iface // 2 // depth
    chunks = slots * per_slot

    def chunk(c):
        first = pl.multiple_of(part * (iface // 2) + (c % per_slot) * depth, depth)
        return pltpu.make_async_copy(
            flex_ref.at[0, 0, c // per_slot, pl.ds(first, depth), :], buffer.at[c % BUFFERS], sem.at[c % BUFFERS]
        )

    def begin():
        for c in range(min(BUFFERS, chunks)):
            chunk(c).start()

    def one(c, carry):
        chunk(c).wait()
        rows = pl.ds(pl.multiple_of((c % per_slot) * depth, depth), depth)
        large, small = pieces(buffer[c % BUFFERS], 2)
        large_ref[c // per_slot, rows, :] = large
        small_ref[c // per_slot, rows, :] = small

        @pl.when(c + BUFFERS < chunks)
        def _():
            chunk(c + BUFFERS).start()

        return carry

    return begin, lambda slot, slots: lax.fori_loop(slot * per_slot, (slot + slots) * per_slot, one, 0)


def pack_kernel(coupling_ref, map_ref, counts_ref, out_ref, map_buffer, sem):
    slots, corners = coupling_ref.shape[2:4]
    span = out_ref.shape[1]
    copies = [
        pltpu.make_async_copy(
            coupling_ref.at[0, 0, s, :, pl.ds(span, span)], out_ref.at[pl.ds(s * corners, corners), :], sem.at[s]
        )
        for s in range(slots)
    ]
    maps = pltpu.make_async_copy(map_ref, map_buffer, sem.at[slots])
    maps.start()
    for copy in copies:
        copy.start()
    maps.wait()
    numbers = jnp.concatenate([map_buffer[s] for s in range(slots)], axis=0).astype(jnp.float32)
    numbers = jnp.concatenate([numbers, jnp.zeros((slots, LANES - corners), jnp.float32)], axis=1)
    live = jnp.full((slots, span - LANES), counts_ref[0, 0], jnp.int32).astype(jnp.float32)
    rest = out_ref.shape[0] - slots * corners - slots
    numbers = jnp.concatenate([jnp.concatenate([numbers, live], axis=1), jnp.zeros((rest, span), jnp.float32)], axis=0)
    out_ref[slots * corners :, :] = numbers
    for copy in copies:
        copy.wait()


def without_numbers(packed, used):
    row = lax.broadcasted_iota(jnp.int32, packed.shape, 0)
    return jnp.where(row < used, packed, 0.0)


def prepare_kernel(
    info_ref, flex_ref, coupling_ref, dof_ref, right_ref, weight_ref, large_ref, small_ref, inverse_ref, dof_rows_ref, link_ref,
    link_t_ref, right_rows_ref, weight_rows_ref, buffer, coupling_buffer, dof_buffer, right_buffer, weight_buffer, flex_sem, sem,
):
    slots, links, width = dof_buffer.shape
    span = links * width
    begin, end = split_in_turn(flex_ref, 0, large_ref, small_ref, buffer, flex_sem)
    others = [
        pltpu.make_async_copy(dof_ref.at[0, 0], dof_buffer, sem.at[0]),
        pltpu.make_async_copy(coupling_ref.at[0, 0], coupling_buffer, sem.at[1]),
        pltpu.make_async_copy(right_ref.at[0, 0], right_buffer, sem.at[2]),
        pltpu.make_async_copy(weight_ref.at[0, 0], weight_buffer, sem.at[3]),
    ]
    for copy in others:
        copy.start()
    begin()
    others[0].wait()
    for j in range(slots):
        for k in range(links):
            at = slice(j * links + k, j * links + k + 1)
            met = dof_buffer[j, k : k + 1, :]
            hit = jnp.broadcast_to(met, (width, width)) == lax.broadcasted_iota(jnp.int32, (width, width), 0)
            place = jnp.where(hit, lax.broadcasted_iota(jnp.int32, (width, width), 1), 0).astype(jnp.float32)
            found = jnp.sum(place.T, axis=0, keepdims=True)
            inverse_ref[at, :] = found.astype(jnp.int32)
            dof_rows_ref[at, :] = met
    others[1].wait()
    link = corner_rows(coupling_buffer[...], span)
    link_ref[...] = stacked(link, 2)
    link_t_ref[...] = jnp.concatenate(pieces(link.T, 2), axis=1)
    others[2].wait()
    others[3].wait()
    for j in range(slots):
        for k in range(links):
            lanes = slice(k * width, (k + 1) * width)
            right_rows_ref[j, :, lanes] = right_buffer[j, :, k, :]
            weight_rows_ref[j : j + 1, lanes] = weight_buffer[j, k : k + 1, :]
    end(0, slots)


def beside(x):
    half = x.shape[0] // 2
    return jnp.concatenate([x[:half], x[half:]], axis=1)


def stacked_again(x):
    half = x.shape[1] // 2
    return jnp.concatenate([x[:, :half], x[:, half:]], axis=0)


def lane_pair(column, at):
    half = column.shape[0] // 2
    lane = lax.broadcasted_iota(jnp.int32, (half, LANES), 1)
    return jnp.where(lane == at, column[:half], jnp.where(lane == at + 1, column[half:], 0.0))


def column_of(tile, at):
    return jnp.concatenate([tile[:, at : at + 1], tile[:, at + 1 : at + 2]], axis=0)


def start_exchange(
    z, norm, partner_ref, inverse_ref, link_t_ref, prev_t_ref, scatter_ref, parity, corners, send_ref, mine_ref, other_ref
):
    slots, loads, span = z.shape
    links = span // LANES
    for j in range(slots):
        for k in range(links):
            block = z[j, :, k * LANES : (k + 1) * LANES]
            index = jnp.broadcast_to(inverse_ref[j * links + k][None], (loads, LANES))
            send_ref[partner_ref[0, 0, k, j], :, k * LANES : (k + 1) * LANES] = -jnp.take_along_axis(block, index, axis=1)
    own = to_corners(z, link_t_ref[...], corners)
    prev = to_corners(send_ref[...], prev_t_ref[...], corners)
    load = through_table(jnp.concatenate([own, prev], axis=1), scatter_ref[...])
    half = load.shape[1] // 2
    low, high = beside(load[:, :half]), beside(load[:, half:])
    spare = lane_pair(norm, 0)
    mine_ref[:, : 2 * half] = jnp.where(parity == 0, low, high)
    other_ref[:, : 2 * half] = jnp.where(parity == 0, high, low)
    mine_ref[:, 2 * half :] = spare
    other_ref[:, 2 * half :] = spare


def local_norm(r, z):
    return jnp.sum(jnp.sum(r * z, axis=0), axis=1, keepdims=True)


def first_kernel(
    corners, info_ref, partner_ref, counts_ref, right_ref, weight_ref, inverse_ref, link_t_ref, map_ref, prev_ref,
    mask_ref, r_ref, z_ref, send_ref, mine_ref, other_ref, prev_t_ref, scatter_ref,
):
    slots, loads, span = r_ref.shape
    links = span // LANES
    used = slots * corners
    live_prev = prev_ref[used : used + 1, LANES : LANES + 1]
    for j in range(slots):
        live = jnp.where(j < counts_ref[0, 0], live_prev, 0.0)
        for k in range(links):
            met = jnp.full((1, LANES), partner_ref[0, 0, k, j], jnp.int32).astype(jnp.float32)
            mask_ref[j : j + 1, k * LANES : (k + 1) * LANES] = jnp.where(met < live, 1.0, 0.0)
    r = right_ref[...] * mask_ref[...][:, None, :]
    z = weight_ref[...][:, None, :] * r
    r_ref[...] = r
    z_ref[...] = z
    prev_t_ref[...] = jnp.concatenate(pieces(without_numbers(prev_ref[...], used).T, 2), axis=1)
    size = scatter_ref.shape[1]
    lane = lax.broadcasted_iota(jnp.int32, (corners, size), 1)
    own = jnp.concatenate([map_ref[j] for j in range(slots)], axis=0).astype(jnp.float32)
    own = jnp.concatenate([own, jnp.zeros((slots, LANES - corners), jnp.float32)], axis=1)
    both = jnp.concatenate([own, prev_ref[used : used + slots, :LANES]], axis=0)
    both = jnp.concatenate([both, jnp.zeros((16 - 2 * slots, LANES), jnp.float32)], axis=0).T
    own = [both[:corners, j : j + 1] for j in range(slots)]
    prev = [both[:corners, slots + j : slots + j + 1] for j in range(slots)]
    for side, columns in enumerate((own, prev)):
        parts = [(c.astype(jnp.int32) == lane).astype(jnp.float32) for c in columns]
        if slots * corners < LANES:
            parts.append(jnp.zeros((LANES - slots * corners, size), jnp.float32))
        scatter_ref[side * LANES : (side + 1) * LANES, :] = jnp.concatenate(parts, axis=0).astype(jnp.bfloat16)
    start_exchange(
        z, local_norm(r, z), partner_ref, inverse_ref, link_t_ref, prev_t_ref, scatter_ref, info_ref[0], corners,
        send_ref, mine_ref, other_ref,
    )


def table_kernel(rows, levels, info_ref, packed_ref, map_ref, *refs):
    *parts, prev_ref, pick_ref, coarse_ref, joined_ref = refs
    slots, _, corners = map_ref.shape
    used = slots * corners
    prev_ref[...] = stacked(without_numbers(packed_ref[...], used), 2)
    side_rows = len(parts) // 2
    per_level = rows * len(parts)
    lines = []
    own = [map_ref[s] for s in range(slots)]
    prev = [packed_ref[used + s : used + s + 1, :corners].astype(jnp.int32) for s in range(slots)]
    for line in (own, prev):
        if slots * corners < LANES:
            line.append(jnp.full((1, LANES - slots * corners), -1, jnp.int32))
        lines += line
    maps = jnp.concatenate(lines, axis=1)
    row = maps // (2 * rows * levels)
    rest = maps - row * (2 * rows * levels)
    level = rest // (2 * rows)
    within = rest - level * (2 * rows)
    place = jnp.bitwise_xor(level, info_ref[2]) * per_level + row * (2 * rows) + within
    place = jnp.where(maps >= 0, place, -1)
    pick_ref[...] = (place == lax.broadcasted_iota(jnp.int32, pick_ref.shape, 0)).astype(jnp.bfloat16)
    for core in range(2):
        for away in range(side_rows):
            at = jnp.bitwise_xor(info_ref[1], away) * (2 * rows) + jnp.bitwise_xor(info_ref[0], core) * rows
            joined_ref[pl.ds(pl.multiple_of(at, 8), rows), :] = parts[core * side_rows + away][...]
    coarse_ref[...] = jnp.concatenate(pieces(joined_ref[...].T, 2), axis=1)


def step_kernel(
    corners, levels, first, last, info_ref, partner_ref, own_ref, facing_ref, weight_ref, dof_ref,
    inverse_ref, mask_ref, link_ref, prev_ref, link_t_ref, prev_t_ref, scatter_ref, pick_ref, r_ref, z_ref, *refs,
):
    refs = list(refs)
    block_refs = refs[:levels]
    refs = refs[levels:]
    if not first:
        x_ref, p_ref, s_ref, past_ref = refs[:4]
        refs = refs[4:]
    x_out, r_out = refs[:2]
    far_ref = refs[-1]
    slots, loads, span = own_ref.shape
    links = span // LANES
    per_level = pick_ref.shape[0] // levels
    spare = block_refs[0][:, 2 * per_level :]
    norm = column_of(spare, 2)
    for ref in block_refs[1:]:
        spare = spare + ref[:, 2 * per_level :]
    product = column_of(spare, 0)
    gathered = jnp.concatenate([stacked_again(ref[:, : 2 * per_level]) for ref in block_refs], axis=1)
    picked = through_table(gathered, pick_ref[...])
    near = own_ref[...] + from_corners(picked[:, :LANES], link_ref[...], slots, corners)
    far_ref[...] = facing_ref[...] + from_corners(picked[:, LANES:], prev_ref[...], slots, corners)
    jumps = []
    for j in range(slots):
        parts = []
        for k in range(links):
            block = far_ref[partner_ref[0, 0, k, j], :, k * LANES : (k + 1) * LANES]
            index = jnp.broadcast_to(dof_ref[j * links + k][None], (loads, LANES))
            parts.append(jnp.take_along_axis(block, index, axis=1))
        jumps.append(jnp.concatenate(parts, axis=1)[None])
    image = (near - jnp.concatenate(jumps, axis=0)) * mask_ref[...][:, None, :]
    if first:
        alpha = norm / product
        p, s = z_ref[...], image
        x = alpha[None] * p
    else:
        ratio = norm / past_ref[:, :1]
        alpha = norm / (product - ratio * norm / past_ref[:, 1:2])
        p = z_ref[...] + ratio[None] * p_ref[...]
        s = image + ratio[None] * s_ref[...]
        x = x_ref[...] + alpha[None] * p
    r = r_ref[...] - alpha[None] * s
    if last:
        for j in range(slots):
            for k in range(links):
                x_out[0, 0, j, :, k, :] = x[j, :, k * LANES : (k + 1) * LANES]
                r_out[0, 0, j, :, k, :] = r[j, :, k * LANES : (k + 1) * LANES]
        return
    z_out, p_out, s_out, past_out, send_ref, mine_ref, other_ref = refs[2:9]
    x_out[...] = x
    r_out[...] = r
    z = weight_ref[...][:, None, :] * r
    z_out[...] = z
    p_out[...] = p
    s_out[...] = s
    lane = lax.broadcasted_iota(jnp.int32, past_out.shape, 1)
    past_out[...] = jnp.where(lane == 0, norm, alpha)
    start_exchange(
        z, local_norm(r, z), partner_ref, inverse_ref, link_t_ref, prev_t_ref, scatter_ref, info_ref[0], corners,
        send_ref, mine_ref, other_ref,
    )


def flex_product(values, large, small):
    loads = values.shape[0]
    full = matmul(stacked(values, 2), large)
    rest = matmul(values.astype(jnp.bfloat16), small)
    return (full[loads:] + rest) + full[:loads]


def flex_near_kernel(values_ref, large_ref, small_ref, out_ref):
    slots, _, width = values_ref.shape
    for s in range(slots):
        out_ref[s] = flex_product(values_ref[s], large_ref[s], small_ref[s])


def flex_far_slot(s, begun, values_ref, forces_ref, large_ref, small_ref, own_ref, facing_ref):
    width = values_ref.shape[2]
    answer = begun + flex_product(forces_ref[s], large_ref[s], small_ref[s])
    own, facing = answer[:, :width], answer[:, width:]
    own_ref[s] = own
    facing_ref[s] = facing
    return jnp.sum(values_ref[s] * own + forces_ref[s] * facing, axis=1, keepdims=True)


def write_energy(work, energy_ref):
    half = energy_ref.shape[1] - LANES
    energy_ref[:, :half] = jnp.zeros((energy_ref.shape[0], half), jnp.float32)
    energy_ref[:, half:] = lane_pair(work, 2)


def flex_far_kernel(values_ref, forces_ref, begun_ref, large_ref, small_ref, own_ref, facing_ref, energy_ref):
    slots, loads, _ = values_ref.shape
    work = jnp.zeros((loads, 1), jnp.float32)
    for s in range(slots):
        work += flex_far_slot(s, begun_ref[s], values_ref, forces_ref, large_ref, small_ref, own_ref, facing_ref)
    write_energy(work, energy_ref)


def flex_first_kernel(
    values_ref, forces_ref, near_large_ref, near_small_ref, flex_ref, own_ref, facing_ref, energy_ref, large_ref, small_ref,
    begun_ref, buffer, sem,
):
    slots, loads, _ = values_ref.shape
    begin, end = split_in_turn(flex_ref, 1, large_ref, small_ref, buffer, sem)
    begin()
    flex_near_kernel(values_ref, near_large_ref, near_small_ref, begun_ref)
    work = jnp.zeros((loads, 1), jnp.float32)
    for s in range(slots):
        end(s, 1)
        work += flex_far_slot(s, begun_ref[s], values_ref, forces_ref, large_ref, small_ref, own_ref, facing_ref)
    write_energy(work, energy_ref)


def coarse_kernel(rows, levels, info_ref, mine_ref, other_ref, table_ref, out_ref):
    parity = info_ref[0]
    half = mine_ref.shape[1] - LANES
    mine, other = stacked_again(mine_ref[:, :half]), stacked_again(other_ref[:, :half])
    low, high = jnp.where(parity == 0, mine, other), jnp.where(parity == 0, other, mine)
    load = jnp.concatenate([low, high], axis=1)
    loads, size = load.shape
    per_level = table_ref.shape[1] // 2
    full = matmul(stacked(load, 3), table_ref[...])

    def part(i, j):
        return full[i * loads : (i + 1) * loads, j * per_level : (j + 1) * per_level]

    answer = ((part(2, 0) + part(1, 1)) + (part(1, 0) + part(0, 1))) + part(0, 0)
    stretch = 2 * rows
    own = jnp.zeros((loads, per_level), jnp.float32)
    for level in range(levels):
        starts = range(level * stretch, size, levels * stretch)
        own = jnp.where(info_ref[2] == level, jnp.concatenate([load[:, a : a + stretch] for a in starts], axis=1), own)
    spare = mine_ref[:, half:]
    product = jnp.sum(answer * own, axis=1, keepdims=True) + column_of(spare + other_ref[:, half:], 2)
    out_ref[:, : 2 * per_level] = beside(answer)
    out_ref[:, 2 * per_level :] = lane_pair(product, 0) + lane_pair(column_of(spare, 0), 2)


VMEM = pl.BlockSpec(memory_space=pltpu.VMEM)
SMEM = pl.BlockSpec(memory_space=pltpu.SMEM)
HBM = pl.BlockSpec(memory_space=pltpu.HBM)
LITTLE = pl.CostEstimate(flops=1024, bytes_accessed=1024, transcendentals=0)
PARAMS = pltpu.CompilerParams(vmem_limit_bytes=14 * 1024 * 1024)


def shape_of(*dims, dtype=jnp.float32):
    return pltpu.VMEM(dims, dtype)


def gathered_along(blocks, bits):
    if len(bits) == 2 and len(blocks) == 1:
        return blocks + [swapped(blocks[0], b) for b in (bits[0], bits[1], bits[0] + bits[1])]
    for bit in bits:
        blocks = blocks + [swapped(b, bit) for b in blocks]
    return blocks


def summed_along(total, bits):
    if len(bits) == 2:
        return sum([swapped(total, b) for b in (bits[0], bits[1], bits[0] + bits[1])], total)
    for bit in bits:
        total = total + swapped(total, bit)
    return total


def powers(start, stop):
    out = []
    while start < stop:
        out.append(start)
        start *= 2
    return out


def local(
    flexibility,
    coupling,
    coarse_inverse,
    precon_weight,
    right_side,
    counts,
    partner,
    dof_index,
    corner_map,
):
    devices, columns = lax.axis_size(BOTH), lax.axis_size("col")
    levels = columns // 2
    slots, iface = flexibility.shape[2:4]
    links, width = dof_index.shape[-2:]
    loads = right_side.shape[3]
    corners = corner_map.shape[-1]
    rows, coarse_size = coarse_inverse.shape
    span = links * width
    per_level = coarse_size // levels
    row_bits, level_bits = powers(columns, devices), powers(2, columns)
    at_col = lax.axis_index("col")
    info = jnp.stack([at_col % 2, lax.axis_index("row"), at_col // 2]).astype(jnp.int32)

    own_map = corner_map.reshape(slots, 1, corners)
    coupling = pltpu.with_memory_space_constraint(coupling, pltpu.HBM)
    to_next = pl.pallas_call(
        pack_kernel,
        out_shape=shape_of(LANES, span),
        in_specs=[HBM, HBM, SMEM],
        out_specs=VMEM,
        scratch_shapes=[pltpu.VMEM((slots, 1, corners), jnp.int32), pltpu.SemaphoreType.DMA((slots + 1,))],
        compiler_params=PARAMS,
        cost_estimate=LITTLE,
        name="pack",
    )(coupling, pltpu.with_memory_space_constraint(own_map, pltpu.HBM), counts)
    coarse_inverse, to_next = lax.optimization_barrier((coarse_inverse, to_next))
    prev_coupling = shifted(to_next, "col", 1)
    coarse_parts = gathered_along([coarse_inverse], row_bits)
    prev_coupling, *coarse_parts[1:3] = lax.optimization_barrier((prev_coupling, *coarse_parts[1:3]))
    coarse_parts = coarse_parts + [swapped(part, 1) for part in coarse_parts]

    state = shape_of(slots, loads, span)
    small = shape_of(loads, LANES)
    half_load = shape_of(loads // 2, coarse_size + LANES)
    out_state = jax.ShapeDtypeStruct(right_side.shape, jnp.float32)

    def table(*dims):
        return shape_of(*dims, dtype=jnp.bfloat16)

    depth = iface // 4
    half_pieces = (table(slots, span, iface), table(slots, span, iface))
    buffers = [pltpu.VMEM((BUFFERS, depth, iface), jnp.float32)]
    flex = pltpu.with_memory_space_constraint(flexibility, pltpu.HBM)
    in_place = [pltpu.with_memory_space_constraint(a, pltpu.HBM) for a in (dof_index, right_side, precon_weight)]
    near_large, near_small, inverse, dof, link, link_t, right, weight = pl.pallas_call(
        prepare_kernel,
        out_shape=half_pieces
        + (
            shape_of(slots * links, width, dtype=jnp.int32), shape_of(slots * links, width, dtype=jnp.int32),
            table(2 * LANES, span), table(span, 2 * LANES), state, shape_of(slots, span),
        ),
        in_specs=[SMEM] + [HBM] * 5,
        out_specs=[VMEM] * 8,
        scratch_shapes=buffers
        + [
            pltpu.VMEM(coupling.shape[2:], jnp.float32),
            pltpu.VMEM((slots, links, width), jnp.int32),
            pltpu.VMEM(right_side.shape[2:], jnp.float32),
            pltpu.VMEM((slots, links, width), jnp.float32),
            pltpu.SemaphoreType.DMA((BUFFERS,)),
            pltpu.SemaphoreType.DMA((4,)),
        ],
        compiler_params=PARAMS,
        cost_estimate=LITTLE,
        name="prepare",
    )(info, flex, coupling, *in_place)
    mask, r, z, send, mine, other, prev_t, scatter = pl.pallas_call(
        functools.partial(first_kernel, corners),
        out_shape=(
            shape_of(slots, span), state, state, state, half_load, half_load, table(span, 2 * LANES),
            table(2 * LANES, coarse_size),
        ),
        in_specs=[SMEM] * 3 + [VMEM] * 6,
        out_specs=[VMEM] * 8,
        compiler_params=PARAMS,
        cost_estimate=LITTLE,
        name="first",
    )(info, partner, counts, right, weight, inverse, link_t, own_map, prev_coupling)

    def tables():
        return pl.pallas_call(
            functools.partial(table_kernel, rows, levels),
            out_shape=(table(2 * LANES, span), table(coarse_size, 2 * LANES), table(coarse_size, 2 * per_level)),
            in_specs=[SMEM] + [VMEM] * (2 + len(coarse_parts)),
            out_specs=[VMEM] * 3,
            scratch_shapes=[pltpu.VMEM((per_level, coarse_size), jnp.float32)],
            compiler_params=pltpu.CompilerParams(vmem_limit_bytes=max(14 * 1024 * 1024, 16 * per_level * coarse_size)),
            cost_estimate=LITTLE,
            name="tables",
        )(info, prev_coupling, own_map, *coarse_parts)

    kept = ()
    for iteration in range(ITERS):
        first, last = iteration == 0, iteration + 1 == ITERS
        forces = shifted(send, "col", -1)
        total = mine + swapped(other, 1)
        if first:
            total = summed_along(total, level_bits)
            own, facing, energy, far_large, far_small = pl.pallas_call(
                flex_first_kernel,
                out_shape=(state, state, half_load) + half_pieces,
                in_specs=[VMEM] * 4 + [HBM],
                out_specs=[VMEM] * 5,
                scratch_shapes=[pltpu.VMEM((slots, loads, iface), jnp.float32)] + buffers + [pltpu.SemaphoreType.DMA((BUFFERS,))],
                compiler_params=PARAMS,
                cost_estimate=LITTLE,
                name="flex_first",
            )(z, forces, near_large, near_small, flex)
        else:
            begun = pl.pallas_call(
                flex_near_kernel,
                out_shape=shape_of(slots, loads, iface),
                in_specs=[VMEM] * 3,
                out_specs=VMEM,
                compiler_params=PARAMS,
                cost_estimate=LITTLE,
                name="flex_near",
            )(z, near_large, near_small)
            total = summed_along(total, level_bits)
            own, facing, energy = pl.pallas_call(
                flex_far_kernel,
                out_shape=(state, state, half_load),
                in_specs=[VMEM] * 5,
                out_specs=[VMEM] * 3,
                compiler_params=PARAMS,
                cost_estimate=LITTLE,
                name="flex_far",
            )(z, forces, begun, far_large, far_small)
        total = summed_along(total + energy, row_bits)
        rest = swapped(total, 1)
        facing_prev = shifted(facing, "col", 1)
        if first:
            prev, pick, coarse_table = tables()
        block = pl.pallas_call(
            functools.partial(coarse_kernel, rows, levels),
            out_shape=shape_of(loads // 2, 2 * per_level + LANES),
            in_specs=[SMEM] + [VMEM] * 3,
            out_specs=VMEM,
            compiler_params=PARAMS,
            cost_estimate=LITTLE,
            name="coarse",
        )(info, total, rest, coarse_table)
        blocks = gathered_along([block], level_bits)
        outs = (out_state, out_state) if last else (state,) * 5 + (small, state, half_load, half_load)
        results = pl.pallas_call(
            functools.partial(step_kernel, corners, levels, first, last),
            out_shape=outs,
            in_specs=[SMEM, SMEM] + [VMEM] * (14 + levels + len(kept)),
            out_specs=[VMEM] * len(outs),
            scratch_shapes=[pltpu.VMEM((slots, loads, span), jnp.float32)],
            compiler_params=PARAMS,
            cost_estimate=LITTLE,
            name="step",
        )(
            info, partner, own, facing_prev, weight, dof, inverse, mask, link, prev, link_t, prev_t,
            scatter, pick, r, z, *blocks, *kept,
        )
        if last:
            return results
        x, r, z, p, s, past, send, mine, other = results
        kept = (x, p, s, past)


def solution(mesh):
    in_specs = (
        P("row", "col", None, None, None),
        P("row", "col", None, None, None),
        P(("row", "col"), None),
        P("row", "col", None, None, None),
        P("row", "col", None, None, None, None),
        P("row", "col"),
        P("row", "col", None, None),
        P("row", "col", None, None, None),
        P("row", "col", None, None),
    )
    out_specs = (P("row", "col", None, None, None, None), P("row", "col", None, None, None, None))
    return jax.shard_map(local, mesh=mesh, in_specs=in_specs, out_specs=out_specs, check_vma=False)
```

```python
import functools
import jax
import jax.numpy as jnp
from jax import lax
from jax.experimental import pallas as pl
from jax.experimental.pallas import tpu as pltpu
from jax.sharding import PartitionSpec as P

ITERS = 3
BOTH = ("row", "col")
LANES = 128
BUFFERS = 6


def shifted(x, axis, by):
    devices = lax.axis_size(axis)
    return lax.ppermute(x, axis, [(i, (i + by) % devices) for i in range(devices)])


def swapped(x, bits):
    devices = lax.axis_size(BOTH)
    return lax.ppermute(x, BOTH, [(i, i ^ bits) for i in range(devices)])


def pieces(x, count):
    out = []
    for step in range(count):
        part = x.astype(jnp.bfloat16)
        out.append(part)
        if step + 1 < count:
            x = x - part.astype(jnp.float32)
    return out


def stacked(x, count):
    return jnp.concatenate(pieces(x, count), axis=0)


def matmul(a, b):
    return jnp.dot(a, b, preferred_element_type=jnp.float32)


def through_table(x, table):
    rows = x.shape[0]
    full = matmul(stacked(x, 3), table)
    return full[2 * rows :] + full[rows : 2 * rows] + full[:rows]


def slot_mask(slots, loads, corners):
    row = lax.broadcasted_iota(jnp.int32, (slots * loads, LANES), 0) // loads
    lane = lax.broadcasted_iota(jnp.int32, (slots * loads, LANES), 1) // corners
    return row == lane


def to_corners(values, columns, corners):
    slots, loads, n = values.shape
    rows = slots * loads
    full = matmul(stacked(values.reshape(rows, n), 2), columns)
    full = (full[rows:, :LANES] + full[:rows, LANES:]) + full[:rows, :LANES]
    kept = jnp.where(slot_mask(slots, loads, corners), full, 0.0)
    return jnp.sum(kept.reshape(slots, loads, LANES), axis=0)


def from_corners(answer, matrix, slots, corners):
    loads = answer.shape[0]
    rows = slots * loads
    spread = jnp.broadcast_to(answer[None], (slots, loads, LANES)).reshape(rows, LANES)
    spread = jnp.where(slot_mask(slots, loads, corners), spread, 0.0)
    both = stacked(spread, 2)
    full = matmul(jnp.concatenate([both, both], axis=1), matrix)
    return (full[rows:] + full[:rows]).reshape(slots, loads, full.shape[1])


def corner_rows(coupling, width):
    slots, corners, _ = coupling.shape
    parts = [coupling[s, :, :width] for s in range(slots)]
    if slots * corners < LANES:
        parts.append(jnp.zeros((LANES - slots * corners, width), jnp.float32))
    return jnp.concatenate(parts, axis=0)


def split_in_turn(flex_ref, part, large_ref, small_ref, buffer, sem):
    slots, iface = flex_ref.shape[2:4]
    depth = buffer.shape[1]
    per_slot = iface // 2 // depth
    chunks = slots * per_slot

    def chunk(c):
        first = pl.multiple_of(part * (iface // 2) + (c % per_slot) * depth, depth)
        return pltpu.make_async_copy(
            flex_ref.at[0, 0, c // per_slot, pl.ds(first, depth), :], buffer.at[c % BUFFERS], sem.at[c % BUFFERS]
        )

    def begin():
        for c in range(min(BUFFERS, chunks)):
            chunk(c).start()

    def one(c, carry):
        chunk(c).wait()
        rows = pl.ds(pl.multiple_of((c % per_slot) * depth, depth), depth)
        large, small = pieces(buffer[c % BUFFERS], 2)
        large_ref[c // per_slot, rows, :] = large
        small_ref[c // per_slot, rows, :] = small

        @pl.when(c + BUFFERS < chunks)
        def _():
            chunk(c + BUFFERS).start()

        return carry

    return begin, lambda slot, slots: lax.fori_loop(slot * per_slot, (slot + slots) * per_slot, one, 0)


def pack_kernel(coupling_ref, map_ref, counts_ref, out_ref, map_buffer, sem):
    slots, corners = coupling_ref.shape[2:4]
    span = out_ref.shape[1]
    copies = [
        pltpu.make_async_copy(
            coupling_ref.at[0, 0, s, :, pl.ds(span, span)], out_ref.at[pl.ds(s * corners, corners), :], sem.at[s]
        )
        for s in range(slots)
    ]
    maps = pltpu.make_async_copy(map_ref, map_buffer, sem.at[slots])
    maps.start()
    for copy in copies:
        copy.start()
    maps.wait()
    numbers = jnp.concatenate([map_buffer[s] for s in range(slots)], axis=0).astype(jnp.float32)
    numbers = jnp.concatenate([numbers, jnp.zeros((slots, LANES - corners), jnp.float32)], axis=1)
    live = jnp.full((slots, span - LANES), counts_ref[0, 0], jnp.int32).astype(jnp.float32)
    rest = out_ref.shape[0] - slots * corners - slots
    numbers = jnp.concatenate([jnp.concatenate([numbers, live], axis=1), jnp.zeros((rest, span), jnp.float32)], axis=0)
    out_ref[slots * corners :, :] = numbers
    for copy in copies:
        copy.wait()


def without_numbers(packed, used):
    row = lax.broadcasted_iota(jnp.int32, packed.shape, 0)
    return jnp.where(row < used, packed, 0.0)


def prepare_kernel(
    info_ref, flex_ref, coupling_ref, dof_ref, right_ref, weight_ref, large_ref, small_ref, inverse_ref, dof_rows_ref, link_ref,
    link_t_ref, right_rows_ref, weight_rows_ref, buffer, coupling_buffer, dof_buffer, right_buffer, weight_buffer, flex_sem, sem,
):
    slots, links, width = dof_buffer.shape
    span = links * width
    begin, end = split_in_turn(flex_ref, 0, large_ref, small_ref, buffer, flex_sem)
    others = [
        pltpu.make_async_copy(dof_ref.at[0, 0], dof_buffer, sem.at[0]),
        pltpu.make_async_copy(coupling_ref.at[0, 0], coupling_buffer, sem.at[1]),
        pltpu.make_async_copy(right_ref.at[0, 0], right_buffer, sem.at[2]),
        pltpu.make_async_copy(weight_ref.at[0, 0], weight_buffer, sem.at[3]),
    ]
    for copy in others:
        copy.start()
    begin()
    others[0].wait()
    for j in range(slots):
        for k in range(links):
            at = slice(j * links + k, j * links + k + 1)
            met = dof_buffer[j, k : k + 1, :]
            hit = jnp.broadcast_to(met, (width, width)) == lax.broadcasted_iota(jnp.int32, (width, width), 0)
            place = jnp.where(hit, lax.broadcasted_iota(jnp.int32, (width, width), 1), 0).astype(jnp.float32)
            found = jnp.sum(place.T, axis=0, keepdims=True)
            inverse_ref[at, :] = found.astype(jnp.int32)
            dof_rows_ref[at, :] = met
    others[1].wait()
    link = corner_rows(coupling_buffer[...], span)
    link_ref[...] = stacked(link, 2)
    link_t_ref[...] = jnp.concatenate(pieces(link.T, 2), axis=1)
    others[2].wait()
    others[3].wait()
    for j in range(slots):
        for k in range(links):
            lanes = slice(k * width, (k + 1) * width)
            right_rows_ref[j, :, lanes] = right_buffer[j, :, k, :]
            weight_rows_ref[j : j + 1, lanes] = weight_buffer[j, k : k + 1, :]
    end(0, slots)


def beside(x):
    half = x.shape[0] // 2
    return jnp.concatenate([x[:half], x[half:]], axis=1)


def stacked_again(x):
    half = x.shape[1] // 2
    return jnp.concatenate([x[:, :half], x[:, half:]], axis=0)


def lane_pair(column, at):
    half = column.shape[0] // 2
    lane = lax.broadcasted_iota(jnp.int32, (half, LANES), 1)
    return jnp.where(lane == at, column[:half], jnp.where(lane == at + 1, column[half:], 0.0))


def column_of(tile, at):
    return jnp.concatenate([tile[:, at : at + 1], tile[:, at + 1 : at + 2]], axis=0)


def start_exchange(
    z, norm, partner_ref, inverse_ref, link_t_ref, prev_t_ref, scatter_ref, parity, corners, send_ref, mine_ref, other_ref
):
    slots, loads, span = z.shape
    links = span // LANES
    for j in range(slots):
        for k in range(links):
            block = z[j, :, k * LANES : (k + 1) * LANES]
            index = jnp.broadcast_to(inverse_ref[j * links + k][None], (loads, LANES))
            send_ref[partner_ref[0, 0, k, j], :, k * LANES : (k + 1) * LANES] = -jnp.take_along_axis(block, index, axis=1)
    own = to_corners(z, link_t_ref[...], corners)
    prev = to_corners(send_ref[...], prev_t_ref[...], corners)
    load = through_table(jnp.concatenate([own, prev], axis=1), scatter_ref[...])
    half = load.shape[1] // 2
    low, high = beside(load[:, :half]), beside(load[:, half:])
    spare = lane_pair(norm, 0)
    mine_ref[:, : 2 * half] = jnp.where(parity == 0, low, high)
    other_ref[:, : 2 * half] = jnp.where(parity == 0, high, low)
    mine_ref[:, 2 * half :] = spare
    other_ref[:, 2 * half :] = spare


def local_norm(r, z):
    return jnp.sum(jnp.sum(r * z, axis=0), axis=1, keepdims=True)


def by_level(numbers, rows, levels):
    row = numbers // (2 * rows * levels)
    rest = numbers - row * (2 * rows * levels)
    level = rest // (2 * rows)
    return level, row * (2 * rows) + rest - level * (2 * rows)


def first_kernel(
    corners, rows, levels, info_ref, partner_ref, counts_ref, right_ref, weight_ref, inverse_ref, link_t_ref, map_ref, prev_ref,
    mask_ref, r_ref, z_ref, send_ref, mine_ref, other_ref, prev_t_ref, scatter_ref,
):
    slots, loads, span = r_ref.shape
    links = span // LANES
    used = slots * corners
    live_prev = prev_ref[used : used + 1, LANES : LANES + 1]
    for j in range(slots):
        live = jnp.where(j < counts_ref[0, 0], live_prev, 0.0)
        for k in range(links):
            met = jnp.full((1, LANES), partner_ref[0, 0, k, j], jnp.int32).astype(jnp.float32)
            mask_ref[j : j + 1, k * LANES : (k + 1) * LANES] = jnp.where(met < live, 1.0, 0.0)
    r = right_ref[...] * mask_ref[...][:, None, :]
    z = weight_ref[...][:, None, :] * r
    r_ref[...] = r
    z_ref[...] = z
    prev_t_ref[...] = jnp.concatenate(pieces(without_numbers(prev_ref[...], used).T, 2), axis=1)
    size = scatter_ref.shape[1]
    lane = lax.broadcasted_iota(jnp.int32, (corners, size), 1)
    own = jnp.concatenate([map_ref[j] for j in range(slots)], axis=0).astype(jnp.float32)
    own = jnp.concatenate([own, jnp.zeros((slots, LANES - corners), jnp.float32)], axis=1)
    both = jnp.concatenate([own, prev_ref[used : used + slots, :LANES]], axis=0)
    both = jnp.concatenate([both, jnp.zeros((16 - 2 * slots, LANES), jnp.float32)], axis=0)
    level, within = by_level(both.astype(jnp.int32), rows, levels)
    both = (level * (size // levels) + within).astype(jnp.float32).T
    own = [both[:corners, j : j + 1] for j in range(slots)]
    prev = [both[:corners, slots + j : slots + j + 1] for j in range(slots)]
    for side, columns in enumerate((own, prev)):
        parts = [(c.astype(jnp.int32) == lane).astype(jnp.float32) for c in columns]
        if slots * corners < LANES:
            parts.append(jnp.zeros((LANES - slots * corners, size), jnp.float32))
        scatter_ref[side * LANES : (side + 1) * LANES, :] = jnp.concatenate(parts, axis=0).astype(jnp.bfloat16)
    start_exchange(
        z, local_norm(r, z), partner_ref, inverse_ref, link_t_ref, prev_t_ref, scatter_ref, info_ref[0], corners,
        send_ref, mine_ref, other_ref,
    )


def table_kernel(rows, levels, info_ref, packed_ref, map_ref, *refs):
    *parts, prev_ref, pick_ref, coarse_ref, joined_ref = refs
    slots, _, corners = map_ref.shape
    used = slots * corners
    prev_ref[...] = stacked(without_numbers(packed_ref[...], used), 2)
    side_rows = len(parts) // 2
    per_level = rows * len(parts)
    lines = []
    own = [map_ref[s] for s in range(slots)]
    prev = [packed_ref[used + s : used + s + 1, :corners].astype(jnp.int32) for s in range(slots)]
    for line in (own, prev):
        if slots * corners < LANES:
            line.append(jnp.full((1, LANES - slots * corners), -1, jnp.int32))
        lines += line
    maps = jnp.concatenate(lines, axis=1)
    level, within = by_level(maps, rows, levels)
    place = jnp.bitwise_xor(level, info_ref[2]) * per_level + within
    place = jnp.where(maps >= 0, place, -1)
    pick_ref[...] = (place == lax.broadcasted_iota(jnp.int32, pick_ref.shape, 0)).astype(jnp.bfloat16)
    for core in range(2):
        for away in range(side_rows):
            at = jnp.bitwise_xor(info_ref[1], away) * (2 * rows) + jnp.bitwise_xor(info_ref[0], core) * rows
            joined_ref[pl.ds(pl.multiple_of(at, 8), rows), :] = parts[core * side_rows + away][...]
    turned = jnp.concatenate(pieces(joined_ref[...].T, 2), axis=1)
    stretch = 2 * rows
    for at in range(side_rows):
        for level in range(levels):
            source = (at * levels + level) * stretch
            target = level * per_level + at * stretch
            coarse_ref[target : target + stretch, :] = turned[source : source + stretch]


def step_kernel(
    corners, levels, first, last, info_ref, partner_ref, own_ref, facing_ref, weight_ref, dof_ref,
    inverse_ref, mask_ref, link_ref, prev_ref, link_t_ref, prev_t_ref, scatter_ref, pick_ref, r_ref, z_ref, *refs,
):
    refs = list(refs)
    block_refs = refs[:levels]
    refs = refs[levels:]
    if not first:
        x_ref, p_ref, s_ref, past_ref = refs[:4]
        refs = refs[4:]
    x_out, r_out = refs[:2]
    far_ref = refs[-1]
    slots, loads, span = own_ref.shape
    links = span // LANES
    per_level = pick_ref.shape[0] // levels
    spare = block_refs[0][:, 2 * per_level :]
    norm = column_of(spare, 2)
    for ref in block_refs[1:]:
        spare = spare + ref[:, 2 * per_level :]
    product = column_of(spare, 0)
    gathered = jnp.concatenate([stacked_again(ref[:, : 2 * per_level]) for ref in block_refs], axis=1)
    picked = through_table(gathered, pick_ref[...])
    near = own_ref[...] + from_corners(picked[:, :LANES], link_ref[...], slots, corners)
    far_ref[...] = facing_ref[...] + from_corners(picked[:, LANES:], prev_ref[...], slots, corners)
    jumps = []
    for j in range(slots):
        parts = []
        for k in range(links):
            block = far_ref[partner_ref[0, 0, k, j], :, k * LANES : (k + 1) * LANES]
            index = jnp.broadcast_to(dof_ref[j * links + k][None], (loads, LANES))
            parts.append(jnp.take_along_axis(block, index, axis=1))
        jumps.append(jnp.concatenate(parts, axis=1)[None])
    image = (near - jnp.concatenate(jumps, axis=0)) * mask_ref[...][:, None, :]
    if first:
        alpha = norm / product
        p, s = z_ref[...], image
        x = alpha[None] * p
    else:
        ratio = norm / past_ref[:, :1]
        alpha = norm / (product - ratio * norm / past_ref[:, 1:2])
        p = z_ref[...] + ratio[None] * p_ref[...]
        s = image + ratio[None] * s_ref[...]
        x = x_ref[...] + alpha[None] * p
    r = r_ref[...] - alpha[None] * s
    if last:
        for j in range(slots):
            for k in range(links):
                x_out[0, 0, j, :, k, :] = x[j, :, k * LANES : (k + 1) * LANES]
                r_out[0, 0, j, :, k, :] = r[j, :, k * LANES : (k + 1) * LANES]
        return
    z_out, p_out, s_out, past_out, send_ref, mine_ref, other_ref = refs[2:9]
    x_out[...] = x
    r_out[...] = r
    z = weight_ref[...][:, None, :] * r
    z_out[...] = z
    p_out[...] = p
    s_out[...] = s
    lane = lax.broadcasted_iota(jnp.int32, past_out.shape, 1)
    past_out[...] = jnp.where(lane == 0, norm, alpha)
    start_exchange(
        z, local_norm(r, z), partner_ref, inverse_ref, link_t_ref, prev_t_ref, scatter_ref, info_ref[0], corners,
        send_ref, mine_ref, other_ref,
    )


def flex_product(values, large, small):
    loads = values.shape[0]
    full = matmul(stacked(values, 2), large)
    rest = matmul(values.astype(jnp.bfloat16), small)
    return (full[loads:] + rest) + full[:loads]


def flex_near_kernel(values_ref, large_ref, small_ref, out_ref):
    slots, _, width = values_ref.shape
    for s in range(slots):
        out_ref[s] = flex_product(values_ref[s], large_ref[s], small_ref[s])


def flex_far_slot(s, begun, values_ref, forces_ref, large_ref, small_ref, own_ref, facing_ref):
    width = values_ref.shape[2]
    answer = begun + flex_product(forces_ref[s], large_ref[s], small_ref[s])
    own, facing = answer[:, :width], answer[:, width:]
    own_ref[s] = own
    facing_ref[s] = facing
    return jnp.sum(values_ref[s] * own + forces_ref[s] * facing, axis=1, keepdims=True)


def write_energy(work, energy_ref):
    half = energy_ref.shape[1] - LANES
    energy_ref[:, :half] = jnp.zeros((energy_ref.shape[0], half), jnp.float32)
    energy_ref[:, half:] = lane_pair(work, 2)


def flex_far_kernel(values_ref, forces_ref, begun_ref, large_ref, small_ref, own_ref, facing_ref, energy_ref):
    slots, loads, _ = values_ref.shape
    work = jnp.zeros((loads, 1), jnp.float32)
    for s in range(slots):
        work += flex_far_slot(s, begun_ref[s], values_ref, forces_ref, large_ref, small_ref, own_ref, facing_ref)
    write_energy(work, energy_ref)


def flex_first_kernel(
    values_ref, forces_ref, near_large_ref, near_small_ref, flex_ref, own_ref, facing_ref, energy_ref, large_ref, small_ref,
    begun_ref, buffer, sem,
):
    slots, loads, _ = values_ref.shape
    begin, end = split_in_turn(flex_ref, 1, large_ref, small_ref, buffer, sem)
    begin()
    flex_near_kernel(values_ref, near_large_ref, near_small_ref, begun_ref)
    work = jnp.zeros((loads, 1), jnp.float32)
    for s in range(slots):
        end(s, 1)
        work += flex_far_slot(s, begun_ref[s], values_ref, forces_ref, large_ref, small_ref, own_ref, facing_ref)
    write_energy(work, energy_ref)


def coarse_kernel(rows, levels, info_ref, mine_ref, other_ref, table_ref, out_ref):
    parity = info_ref[0]
    half = mine_ref.shape[1] - LANES
    mine, other = stacked_again(mine_ref[:, :half]), stacked_again(other_ref[:, :half])
    low, high = jnp.where(parity == 0, mine, other), jnp.where(parity == 0, other, mine)
    load = jnp.concatenate([low, high], axis=1)
    loads, size = load.shape
    per_level = table_ref.shape[1] // 2
    full = matmul(stacked(load, 3), table_ref[...])

    def part(i, j):
        return full[i * loads : (i + 1) * loads, j * per_level : (j + 1) * per_level]

    answer = ((part(2, 0) + part(1, 1)) + (part(1, 0) + part(0, 1))) + part(0, 0)
    own = load[:, :per_level]
    for level in range(1, levels):
        own = jnp.where(info_ref[2] == level, load[:, level * per_level : (level + 1) * per_level], own)
    spare = mine_ref[:, half:]
    product = jnp.sum(answer * own, axis=1, keepdims=True) + column_of(spare + other_ref[:, half:], 2)
    out_ref[:, : 2 * per_level] = beside(answer)
    out_ref[:, 2 * per_level :] = lane_pair(product, 0) + lane_pair(column_of(spare, 0), 2)


VMEM = pl.BlockSpec(memory_space=pltpu.VMEM)
SMEM = pl.BlockSpec(memory_space=pltpu.SMEM)
HBM = pl.BlockSpec(memory_space=pltpu.HBM)
LITTLE = pl.CostEstimate(flops=1024, bytes_accessed=1024, transcendentals=0)
PARAMS = pltpu.CompilerParams(vmem_limit_bytes=14 * 1024 * 1024)


def shape_of(*dims, dtype=jnp.float32):
    return pltpu.VMEM(dims, dtype)


def gathered_along(blocks, bits):
    if len(bits) == 2 and len(blocks) == 1:
        return blocks + [swapped(blocks[0], b) for b in (bits[0], bits[1], bits[0] + bits[1])]
    for bit in bits:
        blocks = blocks + [swapped(b, bit) for b in blocks]
    return blocks


def summed_along(total, bits):
    if len(bits) == 2:
        return sum([swapped(total, b) for b in (bits[0], bits[1], bits[0] + bits[1])], total)
    for bit in bits:
        total = total + swapped(total, bit)
    return total


def powers(start, stop):
    out = []
    while start < stop:
        out.append(start)
        start *= 2
    return out


def local(
    flexibility,
    coupling,
    coarse_inverse,
    precon_weight,
    right_side,
    counts,
    partner,
    dof_index,
    corner_map,
):
    devices, columns = lax.axis_size(BOTH), lax.axis_size("col")
    levels = columns // 2
    slots, iface = flexibility.shape[2:4]
    links, width = dof_index.shape[-2:]
    loads = right_side.shape[3]
    corners = corner_map.shape[-1]
    rows, coarse_size = coarse_inverse.shape
    span = links * width
    per_level = coarse_size // levels
    row_bits, level_bits = powers(columns, devices), powers(2, columns)
    at_col = lax.axis_index("col")
    info = jnp.stack([at_col % 2, lax.axis_index("row"), at_col // 2]).astype(jnp.int32)

    own_map = corner_map.reshape(slots, 1, corners)
    coupling = pltpu.with_memory_space_constraint(coupling, pltpu.HBM)
    to_next = pl.pallas_call(
        pack_kernel,
        out_shape=shape_of(LANES, span),
        in_specs=[HBM, HBM, SMEM],
        out_specs=VMEM,
        scratch_shapes=[pltpu.VMEM((slots, 1, corners), jnp.int32), pltpu.SemaphoreType.DMA((slots + 1,))],
        compiler_params=PARAMS,
        cost_estimate=LITTLE,
        name="pack",
    )(coupling, pltpu.with_memory_space_constraint(own_map, pltpu.HBM), counts)
    coarse_inverse, to_next = lax.optimization_barrier((coarse_inverse, to_next))
    prev_coupling = shifted(to_next, "col", 1)
    coarse_parts = gathered_along([coarse_inverse], row_bits)

    state = shape_of(slots, loads, span)
    small = shape_of(loads, LANES)
    half_load = shape_of(loads // 2, coarse_size + LANES)
    out_state = jax.ShapeDtypeStruct(right_side.shape, jnp.float32)

    def table(*dims):
        return shape_of(*dims, dtype=jnp.bfloat16)

    depth = iface // 4
    half_pieces = (table(slots, span, iface), table(slots, span, iface))
    buffers = [pltpu.VMEM((BUFFERS, depth, iface), jnp.float32)]
    flex = pltpu.with_memory_space_constraint(flexibility, pltpu.HBM)
    in_place = [pltpu.with_memory_space_constraint(a, pltpu.HBM) for a in (dof_index, right_side, precon_weight)]
    near_large, near_small, inverse, dof, link, link_t, right, weight = pl.pallas_call(
        prepare_kernel,
        out_shape=half_pieces
        + (
            shape_of(slots * links, width, dtype=jnp.int32), shape_of(slots * links, width, dtype=jnp.int32),
            table(2 * LANES, span), table(span, 2 * LANES), state, shape_of(slots, span),
        ),
        in_specs=[SMEM] + [HBM] * 5,
        out_specs=[VMEM] * 8,
        scratch_shapes=buffers
        + [
            pltpu.VMEM(coupling.shape[2:], jnp.float32),
            pltpu.VMEM((slots, links, width), jnp.int32),
            pltpu.VMEM(right_side.shape[2:], jnp.float32),
            pltpu.VMEM((slots, links, width), jnp.float32),
            pltpu.SemaphoreType.DMA((BUFFERS,)),
            pltpu.SemaphoreType.DMA((4,)),
        ],
        compiler_params=PARAMS,
        cost_estimate=LITTLE,
        name="prepare",
    )(info, flex, coupling, *in_place)
    mask, r, z, send, mine, other, prev_t, scatter = pl.pallas_call(
        functools.partial(first_kernel, corners, rows, levels),
        out_shape=(
            shape_of(slots, span), state, state, state, half_load, half_load, table(span, 2 * LANES),
            table(2 * LANES, coarse_size),
        ),
        in_specs=[SMEM] * 3 + [VMEM] * 6,
        out_specs=[VMEM] * 8,
        compiler_params=PARAMS,
        cost_estimate=LITTLE,
        name="first",
    )(info, partner, counts, right, weight, inverse, link_t, own_map, prev_coupling)

    def tables():
        return pl.pallas_call(
            functools.partial(table_kernel, rows, levels),
            out_shape=(table(2 * LANES, span), table(coarse_size, 2 * LANES), table(coarse_size, 2 * per_level)),
            in_specs=[SMEM] + [VMEM] * (2 + len(coarse_parts)),
            out_specs=[VMEM] * 3,
            scratch_shapes=[pltpu.VMEM((per_level, coarse_size), jnp.float32)],
            compiler_params=pltpu.CompilerParams(vmem_limit_bytes=max(14 * 1024 * 1024, 16 * per_level * coarse_size)),
            cost_estimate=LITTLE,
            name="tables",
        )(info, prev_coupling, own_map, *coarse_parts)

    kept = ()
    for iteration in range(ITERS):
        first, last = iteration == 0, iteration + 1 == ITERS
        forces = shifted(send, "col", -1)
        if first:
            forces, *coarse_parts[1:] = lax.optimization_barrier((forces, *coarse_parts[1:]))
            coarse_parts += [swapped(part, 1) for part in coarse_parts]
        total = mine + swapped(other, 1)
        if first:
            total = summed_along(total, level_bits)
            own, facing, energy, far_large, far_small = pl.pallas_call(
                flex_first_kernel,
                out_shape=(state, state, half_load) + half_pieces,
                in_specs=[VMEM] * 4 + [HBM],
                out_specs=[VMEM] * 5,
                scratch_shapes=[pltpu.VMEM((slots, loads, iface), jnp.float32)] + buffers + [pltpu.SemaphoreType.DMA((BUFFERS,))],
                compiler_params=PARAMS,
                cost_estimate=LITTLE,
                name="flex_first",
            )(z, forces, near_large, near_small, flex)
        else:
            begun = pl.pallas_call(
                flex_near_kernel,
                out_shape=shape_of(slots, loads, iface),
                in_specs=[VMEM] * 3,
                out_specs=VMEM,
                compiler_params=PARAMS,
                cost_estimate=LITTLE,
                name="flex_near",
            )(z, near_large, near_small)
            total = summed_along(total, level_bits)
            own, facing, energy = pl.pallas_call(
                flex_far_kernel,
                out_shape=(state, state, half_load),
                in_specs=[VMEM] * 5,
                out_specs=[VMEM] * 3,
                compiler_params=PARAMS,
                cost_estimate=LITTLE,
                name="flex_far",
            )(z, forces, begun, far_large, far_small)
        total = summed_along(total + energy, row_bits)
        rest = swapped(total, 1)
        facing_prev = shifted(facing, "col", 1)
        if first:
            prev, pick, coarse_table = tables()
        block = pl.pallas_call(
            functools.partial(coarse_kernel, rows, levels),
            out_shape=shape_of(loads // 2, 2 * per_level + LANES),
            in_specs=[SMEM] + [VMEM] * 3,
            out_specs=VMEM,
            compiler_params=PARAMS,
            cost_estimate=LITTLE,
            name="coarse",
        )(info, total, rest, coarse_table)
        blocks = gathered_along([block], level_bits)
        outs = (out_state, out_state) if last else (state,) * 5 + (small, state, half_load, half_load)
        results = pl.pallas_call(
            functools.partial(step_kernel, corners, levels, first, last),
            out_shape=outs,
            in_specs=[SMEM, SMEM] + [VMEM] * (14 + levels + len(kept)),
            out_specs=[VMEM] * len(outs),
            scratch_shapes=[pltpu.VMEM((slots, loads, span), jnp.float32)],
            compiler_params=PARAMS,
            cost_estimate=LITTLE,
            name="step",
        )(
            info, partner, own, facing_prev, weight, dof, inverse, mask, link, prev, link_t, prev_t,
            scatter, pick, r, z, *blocks, *kept,
        )
        if last:
            return results
        x, r, z, p, s, past, send, mine, other = results
        kept = (x, p, s, past)


def solution(mesh):
    in_specs = (
        P("row", "col", None, None, None),
        P("row", "col", None, None, None),
        P(("row", "col"), None),
        P("row", "col", None, None, None),
        P("row", "col", None, None, None, None),
        P("row", "col"),
        P("row", "col", None, None),
        P("row", "col", None, None, None),
        P("row", "col", None, None),
    )
    out_specs = (P("row", "col", None, None, None, None), P("row", "col", None, None, None, None))
    return jax.shard_map(local, mesh=mesh, in_specs=in_specs, out_specs=out_specs, check_vma=False)
```

```python
import functools
import jax
import jax.numpy as jnp
from jax import lax
from jax.experimental import pallas as pl
from jax.experimental.pallas import tpu as pltpu
from jax.sharding import PartitionSpec as P

ITERS = 3
BOTH = ("row", "col")
LANES = 128
BUFFERS = 6


def shifted(x, axis, by):
    devices = lax.axis_size(axis)
    return lax.ppermute(x, axis, [(i, (i + by) % devices) for i in range(devices)])


def swapped(x, bits):
    devices = lax.axis_size(BOTH)
    return lax.ppermute(x, BOTH, [(i, i ^ bits) for i in range(devices)])


def pieces(x, count):
    out = []
    for step in range(count):
        part = x.astype(jnp.bfloat16)
        out.append(part)
        if step + 1 < count:
            x = x - part.astype(jnp.float32)
    return out


def stacked(x, count):
    return jnp.concatenate(pieces(x, count), axis=0)


def matmul(a, b):
    return jnp.dot(a, b, preferred_element_type=jnp.float32)


def through_table(x, table):
    rows = x.shape[0]
    full = matmul(stacked(x, 3), table)
    return full[2 * rows :] + full[rows : 2 * rows] + full[:rows]


def slot_mask(slots, loads, corners):
    row = lax.broadcasted_iota(jnp.int32, (slots * loads, LANES), 0) // loads
    lane = lax.broadcasted_iota(jnp.int32, (slots * loads, LANES), 1) // corners
    return row == lane


def to_corners(values, columns, corners):
    slots, loads, n = values.shape
    rows = slots * loads
    full = matmul(stacked(values.reshape(rows, n), 2), columns)
    full = (full[rows:, :LANES] + full[:rows, LANES:]) + full[:rows, :LANES]
    kept = jnp.where(slot_mask(slots, loads, corners), full, 0.0)
    return jnp.sum(kept.reshape(slots, loads, LANES), axis=0)


def from_corners(answer, matrix, slots, corners):
    loads = answer.shape[0]
    rows = slots * loads
    spread = jnp.broadcast_to(answer[None], (slots, loads, LANES)).reshape(rows, LANES)
    spread = jnp.where(slot_mask(slots, loads, corners), spread, 0.0)
    both = stacked(spread, 2)
    full = matmul(jnp.concatenate([both, both], axis=1), matrix)
    return (full[rows:] + full[:rows]).reshape(slots, loads, full.shape[1])


def corner_rows(coupling, width):
    slots, corners, _ = coupling.shape
    parts = [coupling[s, :, :width] for s in range(slots)]
    if slots * corners < LANES:
        parts.append(jnp.zeros((LANES - slots * corners, width), jnp.float32))
    return jnp.concatenate(parts, axis=0)


def split_in_turn(flex_ref, part, large_ref, small_ref, buffer, sem):
    slots, iface = flex_ref.shape[2:4]
    depth = buffer.shape[1]
    per_slot = iface // 2 // depth
    chunks = slots * per_slot

    def chunk(c):
        first = pl.multiple_of(part * (iface // 2) + (c % per_slot) * depth, depth)
        return pltpu.make_async_copy(
            flex_ref.at[0, 0, c // per_slot, pl.ds(first, depth), :], buffer.at[c % BUFFERS], sem.at[c % BUFFERS]
        )

    def begin():
        for c in range(min(BUFFERS, chunks)):
            chunk(c).start()

    def one(c, carry):
        chunk(c).wait()
        rows = pl.ds(pl.multiple_of((c % per_slot) * depth, depth), depth)
        large, small = pieces(buffer[c % BUFFERS], 2)
        large_ref[c // per_slot, rows, :] = large
        small_ref[c // per_slot, rows, :] = small

        @pl.when(c + BUFFERS < chunks)
        def _():
            chunk(c + BUFFERS).start()

        return carry

    return begin, lambda slot, slots: lax.fori_loop(slot * per_slot, (slot + slots) * per_slot, one, 0)


def pack_kernel(coupling_ref, map_ref, counts_ref, out_ref, map_buffer, sem):
    slots, corners = coupling_ref.shape[2:4]
    span = out_ref.shape[1]
    copies = [
        pltpu.make_async_copy(
            coupling_ref.at[0, 0, s, :, pl.ds(span, span)], out_ref.at[pl.ds(s * corners, corners), :], sem.at[s]
        )
        for s in range(slots)
    ]
    maps = pltpu.make_async_copy(map_ref, map_buffer, sem.at[slots])
    maps.start()
    for copy in copies:
        copy.start()
    maps.wait()
    numbers = jnp.concatenate([map_buffer[s] for s in range(slots)], axis=0).astype(jnp.float32)
    numbers = jnp.concatenate([numbers, jnp.zeros((slots, LANES - corners), jnp.float32)], axis=1)
    live = jnp.full((slots, span - LANES), counts_ref[0, 0], jnp.int32).astype(jnp.float32)
    rest = out_ref.shape[0] - slots * corners - slots
    numbers = jnp.concatenate([jnp.concatenate([numbers, live], axis=1), jnp.zeros((rest, span), jnp.float32)], axis=0)
    out_ref[slots * corners :, :] = numbers
    for copy in copies:
        copy.wait()


def without_numbers(packed, used):
    row = lax.broadcasted_iota(jnp.int32, packed.shape, 0)
    return jnp.where(row < used, packed, 0.0)


def prepare_kernel(
    info_ref, flex_ref, coupling_ref, dof_ref, right_ref, weight_ref, large_ref, small_ref, inverse_ref, dof_rows_ref, link_ref,
    link_t_ref, right_rows_ref, weight_rows_ref, buffer, coupling_buffer, dof_buffer, right_buffer, weight_buffer, flex_sem, sem,
):
    slots, links, width = dof_buffer.shape
    span = links * width
    begin, end = split_in_turn(flex_ref, 0, large_ref, small_ref, buffer, flex_sem)
    others = [
        pltpu.make_async_copy(dof_ref.at[0, 0], dof_buffer, sem.at[0]),
        pltpu.make_async_copy(coupling_ref.at[0, 0], coupling_buffer, sem.at[1]),
        pltpu.make_async_copy(right_ref.at[0, 0], right_buffer, sem.at[2]),
        pltpu.make_async_copy(weight_ref.at[0, 0], weight_buffer, sem.at[3]),
    ]
    for copy in others:
        copy.start()
    begin()
    others[0].wait()
    for j in range(slots):
        for k in range(links):
            at = slice(j * links + k, j * links + k + 1)
            met = dof_buffer[j, k : k + 1, :]
            hit = jnp.broadcast_to(met, (width, width)) == lax.broadcasted_iota(jnp.int32, (width, width), 0)
            place = jnp.where(hit, lax.broadcasted_iota(jnp.int32, (width, width), 1), 0).astype(jnp.float32)
            found = jnp.sum(place.T, axis=0, keepdims=True)
            inverse_ref[at, :] = found.astype(jnp.int32)
            dof_rows_ref[at, :] = met
    end(0, 2)
    others[1].wait()
    link = corner_rows(coupling_buffer[...], span)
    link_ref[...] = stacked(link, 2)
    link_t_ref[...] = jnp.concatenate(pieces(link.T, 2), axis=1)
    end(2, 1)
    others[2].wait()
    others[3].wait()
    for j in range(slots):
        for k in range(links):
            lanes = slice(k * width, (k + 1) * width)
            right_rows_ref[j, :, lanes] = right_buffer[j, :, k, :]
            weight_rows_ref[j : j + 1, lanes] = weight_buffer[j, k : k + 1, :]
    end(3, slots - 3)


def beside(x):
    half = x.shape[0] // 2
    return jnp.concatenate([x[:half], x[half:]], axis=1)


def stacked_again(x):
    half = x.shape[1] // 2
    return jnp.concatenate([x[:, :half], x[:, half:]], axis=0)


def lane_pair(column, at):
    half = column.shape[0] // 2
    lane = lax.broadcasted_iota(jnp.int32, (half, LANES), 1)
    return jnp.where(lane == at, column[:half], jnp.where(lane == at + 1, column[half:], 0.0))


def column_of(tile, at):
    return jnp.concatenate([tile[:, at : at + 1], tile[:, at + 1 : at + 2]], axis=0)


def start_exchange(
    z, norm, partner_ref, inverse_ref, link_t_ref, prev_t_ref, scatter_ref, parity, corners, send_ref, mine_ref, other_ref
):
    slots, loads, span = z.shape
    links = span // LANES
    for j in range(slots):
        for k in range(links):
            block = z[j, :, k * LANES : (k + 1) * LANES]
            index = jnp.broadcast_to(inverse_ref[j * links + k][None], (loads, LANES))
            send_ref[partner_ref[0, 0, k, j], :, k * LANES : (k + 1) * LANES] = -jnp.take_along_axis(block, index, axis=1)
    own = to_corners(z, link_t_ref[...], corners)
    prev = to_corners(send_ref[...], prev_t_ref[...], corners)
    load = through_table(jnp.concatenate([own, prev], axis=1), scatter_ref[...])
    half = load.shape[1] // 2
    low, high = beside(load[:, :half]), beside(load[:, half:])
    spare = lane_pair(norm, 0)
    mine_ref[:, : 2 * half] = jnp.where(parity == 0, low, high)
    other_ref[:, : 2 * half] = jnp.where(parity == 0, high, low)
    mine_ref[:, 2 * half :] = spare
    other_ref[:, 2 * half :] = spare


def local_norm(r, z):
    return jnp.sum(jnp.sum(r * z, axis=0), axis=1, keepdims=True)


def by_level(numbers, rows, levels):
    row = numbers // (2 * rows * levels)
    rest = numbers - row * (2 * rows * levels)
    level = rest // (2 * rows)
    return level, row * (2 * rows) + rest - level * (2 * rows)


def first_kernel(
    corners, rows, levels, info_ref, partner_ref, counts_ref, right_ref, weight_ref, inverse_ref, link_t_ref, map_ref, prev_ref,
    mask_ref, r_ref, z_ref, send_ref, mine_ref, other_ref, prev_t_ref, scatter_ref,
):
    slots, loads, span = r_ref.shape
    links = span // LANES
    used = slots * corners
    live_prev = prev_ref[used : used + 1, LANES : LANES + 1]
    for j in range(slots):
        live = jnp.where(j < counts_ref[0, 0], live_prev, 0.0)
        for k in range(links):
            met = jnp.full((1, LANES), partner_ref[0, 0, k, j], jnp.int32).astype(jnp.float32)
            mask_ref[j : j + 1, k * LANES : (k + 1) * LANES] = jnp.where(met < live, 1.0, 0.0)
    r = right_ref[...] * mask_ref[...][:, None, :]
    z = weight_ref[...][:, None, :] * r
    r_ref[...] = r
    z_ref[...] = z
    prev_t_ref[...] = jnp.concatenate(pieces(without_numbers(prev_ref[...], used).T, 2), axis=1)
    size = scatter_ref.shape[1]
    lane = lax.broadcasted_iota(jnp.int32, (corners, size), 1)
    own = jnp.concatenate([map_ref[j] for j in range(slots)], axis=0).astype(jnp.float32)
    own = jnp.concatenate([own, jnp.zeros((slots, LANES - corners), jnp.float32)], axis=1)
    both = jnp.concatenate([own, prev_ref[used : used + slots, :LANES]], axis=0)
    both = jnp.concatenate([both, jnp.zeros((16 - 2 * slots, LANES), jnp.float32)], axis=0)
    level, within = by_level(both.astype(jnp.int32), rows, levels)
    both = (level * (size // levels) + within).astype(jnp.float32).T
    own = [both[:corners, j : j + 1] for j in range(slots)]
    prev = [both[:corners, slots + j : slots + j + 1] for j in range(slots)]
    for side, columns in enumerate((own, prev)):
        parts = [(c.astype(jnp.int32) == lane).astype(jnp.float32) for c in columns]
        if slots * corners < LANES:
            parts.append(jnp.zeros((LANES - slots * corners, size), jnp.float32))
        scatter_ref[side * LANES : (side + 1) * LANES, :] = jnp.concatenate(parts, axis=0).astype(jnp.bfloat16)
    start_exchange(
        z, local_norm(r, z), partner_ref, inverse_ref, link_t_ref, prev_t_ref, scatter_ref, info_ref[0], corners,
        send_ref, mine_ref, other_ref,
    )


def table_kernel(rows, levels, info_ref, packed_ref, map_ref, *refs):
    *parts, prev_ref, pick_ref, coarse_ref, joined_ref = refs
    slots, _, corners = map_ref.shape
    used = slots * corners
    prev_ref[...] = stacked(without_numbers(packed_ref[...], used), 2)
    side_rows = len(parts) // 2
    per_level = rows * len(parts)
    lines = []
    own = [map_ref[s] for s in range(slots)]
    prev = [packed_ref[used + s : used + s + 1, :corners].astype(jnp.int32) for s in range(slots)]
    for line in (own, prev):
        if slots * corners < LANES:
            line.append(jnp.full((1, LANES - slots * corners), -1, jnp.int32))
        lines += line
    maps = jnp.concatenate(lines, axis=1)
    level, within = by_level(maps, rows, levels)
    place = jnp.bitwise_xor(level, info_ref[2]) * per_level + within
    place = jnp.where(maps >= 0, place, -1)
    pick_ref[...] = (place == lax.broadcasted_iota(jnp.int32, pick_ref.shape, 0)).astype(jnp.bfloat16)
    for core in range(2):
        for away in range(side_rows):
            at = jnp.bitwise_xor(info_ref[1], away) * (2 * rows) + jnp.bitwise_xor(info_ref[0], core) * rows
            joined_ref[pl.ds(pl.multiple_of(at, 8), rows), :] = parts[core * side_rows + away][...]
    turned = jnp.concatenate(pieces(joined_ref[...].T, 2), axis=1)
    stretch = 2 * rows
    for at in range(side_rows):
        for level in range(levels):
            source = (at * levels + level) * stretch
            target = level * per_level + at * stretch
            coarse_ref[target : target + stretch, :] = turned[source : source + stretch]


def step_kernel(
    corners, levels, first, last, info_ref, partner_ref, own_ref, facing_ref, weight_ref, dof_ref,
    inverse_ref, mask_ref, link_ref, prev_ref, link_t_ref, prev_t_ref, scatter_ref, pick_ref, r_ref, z_ref, *refs,
):
    refs = list(refs)
    block_refs = refs[:levels]
    refs = refs[levels:]
    if not first:
        x_ref, p_ref, s_ref, past_ref = refs[:4]
        refs = refs[4:]
    x_out, r_out = refs[:2]
    far_ref = refs[-1]
    slots, loads, span = own_ref.shape
    links = span // LANES
    per_level = pick_ref.shape[0] // levels
    spare = block_refs[0][:, 2 * per_level :]
    norm = column_of(spare, 2)
    for ref in block_refs[1:]:
        spare = spare + ref[:, 2 * per_level :]
    product = column_of(spare, 0)
    gathered = jnp.concatenate([stacked_again(ref[:, : 2 * per_level]) for ref in block_refs], axis=1)
    picked = through_table(gathered, pick_ref[...])
    near = own_ref[...] + from_corners(picked[:, :LANES], link_ref[...], slots, corners)
    far_ref[...] = facing_ref[...] + from_corners(picked[:, LANES:], prev_ref[...], slots, corners)
    jumps = []
    for j in range(slots):
        parts = []
        for k in range(links):
            block = far_ref[partner_ref[0, 0, k, j], :, k * LANES : (k + 1) * LANES]
            index = jnp.broadcast_to(dof_ref[j * links + k][None], (loads, LANES))
            parts.append(jnp.take_along_axis(block, index, axis=1))
        jumps.append(jnp.concatenate(parts, axis=1)[None])
    image = (near - jnp.concatenate(jumps, axis=0)) * mask_ref[...][:, None, :]
    if first:
        alpha = norm / product
        p, s = z_ref[...], image
        x = alpha[None] * p
    else:
        ratio = norm / past_ref[:, :1]
        alpha = norm / (product - ratio * norm / past_ref[:, 1:2])
        p = z_ref[...] + ratio[None] * p_ref[...]
        s = image + ratio[None] * s_ref[...]
        x = x_ref[...] + alpha[None] * p
    r = r_ref[...] - alpha[None] * s
    if last:
        for j in range(slots):
            for k in range(links):
                x_out[0, 0, j, :, k, :] = x[j, :, k * LANES : (k + 1) * LANES]
                r_out[0, 0, j, :, k, :] = r[j, :, k * LANES : (k + 1) * LANES]
        return
    z_out, p_out, s_out, past_out, send_ref, mine_ref, other_ref = refs[2:9]
    x_out[...] = x
    r_out[...] = r
    z = weight_ref[...][:, None, :] * r
    z_out[...] = z
    p_out[...] = p
    s_out[...] = s
    lane = lax.broadcasted_iota(jnp.int32, past_out.shape, 1)
    past_out[...] = jnp.where(lane == 0, norm, alpha)
    start_exchange(
        z, local_norm(r, z), partner_ref, inverse_ref, link_t_ref, prev_t_ref, scatter_ref, info_ref[0], corners,
        send_ref, mine_ref, other_ref,
    )


def flex_product(values, large, small):
    loads = values.shape[0]
    full = matmul(stacked(values, 2), large)
    rest = matmul(values.astype(jnp.bfloat16), small)
    return (full[loads:] + rest) + full[:loads]


def flex_near_kernel(values_ref, large_ref, small_ref, out_ref):
    slots, _, width = values_ref.shape
    for s in range(slots):
        out_ref[s] = flex_product(values_ref[s], large_ref[s], small_ref[s])


def flex_far_slot(s, begun, values_ref, forces_ref, large_ref, small_ref, own_ref, facing_ref):
    width = values_ref.shape[2]
    answer = begun + flex_product(forces_ref[s], large_ref[s], small_ref[s])
    own, facing = answer[:, :width], answer[:, width:]
    own_ref[s] = own
    facing_ref[s] = facing
    return jnp.sum(values_ref[s] * own + forces_ref[s] * facing, axis=1, keepdims=True)


def write_energy(work, energy_ref):
    half = energy_ref.shape[1] - LANES
    energy_ref[:, :half] = jnp.zeros((energy_ref.shape[0], half), jnp.float32)
    energy_ref[:, half:] = lane_pair(work, 2)


def flex_kernel(
    values_ref, forces_ref, near_large_ref, near_small_ref, large_ref, small_ref, own_ref, facing_ref, energy_ref
):
    slots, loads, _ = values_ref.shape
    work = jnp.zeros((loads, 1), jnp.float32)
    for s in range(slots):
        begun = flex_product(values_ref[s], near_large_ref[s], near_small_ref[s])
        work += flex_far_slot(s, begun, values_ref, forces_ref, large_ref, small_ref, own_ref, facing_ref)
    write_energy(work, energy_ref)


def flex_first_kernel(
    values_ref, forces_ref, near_large_ref, near_small_ref, flex_ref, own_ref, facing_ref, energy_ref, large_ref, small_ref,
    begun_ref, buffer, sem,
):
    slots, loads, _ = values_ref.shape
    begin, end = split_in_turn(flex_ref, 1, large_ref, small_ref, buffer, sem)
    begin()
    flex_near_kernel(values_ref, near_large_ref, near_small_ref, begun_ref)
    work = jnp.zeros((loads, 1), jnp.float32)
    for s in range(slots):
        end(s, 1)
        work += flex_far_slot(s, begun_ref[s], values_ref, forces_ref, large_ref, small_ref, own_ref, facing_ref)
    write_energy(work, energy_ref)


def coarse_kernel(rows, levels, info_ref, mine_ref, other_ref, table_ref, out_ref):
    parity = info_ref[0]
    half = mine_ref.shape[1] - LANES
    mine, other = stacked_again(mine_ref[:, :half]), stacked_again(other_ref[:, :half])
    low, high = jnp.where(parity == 0, mine, other), jnp.where(parity == 0, other, mine)
    load = jnp.concatenate([low, high], axis=1)
    loads, size = load.shape
    per_level = table_ref.shape[1] // 2
    full = matmul(stacked(load, 3), table_ref[...])

    def part(i, j):
        return full[i * loads : (i + 1) * loads, j * per_level : (j + 1) * per_level]

    answer = ((part(2, 0) + part(1, 1)) + (part(1, 0) + part(0, 1))) + part(0, 0)
    own = load[:, :per_level]
    for level in range(1, levels):
        own = jnp.where(info_ref[2] == level, load[:, level * per_level : (level + 1) * per_level], own)
    spare = mine_ref[:, half:]
    product = jnp.sum(answer * own, axis=1, keepdims=True) + column_of(spare + other_ref[:, half:], 2)
    out_ref[:, : 2 * per_level] = beside(answer)
    out_ref[:, 2 * per_level :] = lane_pair(product, 0) + lane_pair(column_of(spare, 0), 2)


VMEM = pl.BlockSpec(memory_space=pltpu.VMEM)
SMEM = pl.BlockSpec(memory_space=pltpu.SMEM)
HBM = pl.BlockSpec(memory_space=pltpu.HBM)
LITTLE = pl.CostEstimate(flops=1024, bytes_accessed=1024, transcendentals=0)
PARAMS = pltpu.CompilerParams(vmem_limit_bytes=14 * 1024 * 1024)


def shape_of(*dims, dtype=jnp.float32):
    return pltpu.VMEM(dims, dtype)


def gathered_along(blocks, bits):
    if len(bits) == 2 and len(blocks) == 1:
        return blocks + [swapped(blocks[0], b) for b in (bits[0], bits[1], bits[0] + bits[1])]
    for bit in bits:
        blocks = blocks + [swapped(b, bit) for b in blocks]
    return blocks


def summed_along(total, bits):
    if len(bits) == 2:
        return sum([swapped(total, b) for b in (bits[0], bits[1], bits[0] + bits[1])], total)
    for bit in bits:
        total = total + swapped(total, bit)
    return total


def powers(start, stop):
    out = []
    while start < stop:
        out.append(start)
        start *= 2
    return out


def local(
    flexibility,
    coupling,
    coarse_inverse,
    precon_weight,
    right_side,
    counts,
    partner,
    dof_index,
    corner_map,
):
    devices, columns = lax.axis_size(BOTH), lax.axis_size("col")
    levels = columns // 2
    slots, iface = flexibility.shape[2:4]
    links, width = dof_index.shape[-2:]
    loads = right_side.shape[3]
    corners = corner_map.shape[-1]
    rows, coarse_size = coarse_inverse.shape
    span = links * width
    per_level = coarse_size // levels
    row_bits, level_bits = powers(columns, devices), powers(2, columns)
    at_col = lax.axis_index("col")
    info = jnp.stack([at_col % 2, lax.axis_index("row"), at_col // 2]).astype(jnp.int32)

    own_map = corner_map.reshape(slots, 1, corners)
    coupling = pltpu.with_memory_space_constraint(coupling, pltpu.HBM)
    to_next = pl.pallas_call(
        pack_kernel,
        out_shape=shape_of(LANES, span),
        in_specs=[HBM, HBM, SMEM],
        out_specs=VMEM,
        scratch_shapes=[pltpu.VMEM((slots, 1, corners), jnp.int32), pltpu.SemaphoreType.DMA((slots + 1,))],
        compiler_params=PARAMS,
        cost_estimate=LITTLE,
        name="pack",
    )(coupling, pltpu.with_memory_space_constraint(own_map, pltpu.HBM), counts)
    coarse_inverse, to_next = lax.optimization_barrier((coarse_inverse, to_next))
    prev_coupling = shifted(to_next, "col", 1)
    coarse_parts = gathered_along([coarse_inverse], row_bits)

    state = shape_of(slots, loads, span)
    small = shape_of(loads, LANES)
    half_load = shape_of(loads // 2, coarse_size + LANES)
    out_state = jax.ShapeDtypeStruct(right_side.shape, jnp.float32)

    def table(*dims):
        return shape_of(*dims, dtype=jnp.bfloat16)

    depth = iface // 4
    half_pieces = (table(slots, span, iface), table(slots, span, iface))
    buffers = [pltpu.VMEM((BUFFERS, depth, iface), jnp.float32)]
    flex = pltpu.with_memory_space_constraint(flexibility, pltpu.HBM)
    in_place = [pltpu.with_memory_space_constraint(a, pltpu.HBM) for a in (dof_index, right_side, precon_weight)]
    near_large, near_small, inverse, dof, link, link_t, right, weight = pl.pallas_call(
        prepare_kernel,
        out_shape=half_pieces
        + (
            shape_of(slots * links, width, dtype=jnp.int32), shape_of(slots * links, width, dtype=jnp.int32),
            table(2 * LANES, span), table(span, 2 * LANES), state, shape_of(slots, span),
        ),
        in_specs=[SMEM] + [HBM] * 5,
        out_specs=[VMEM] * 8,
        scratch_shapes=buffers
        + [
            pltpu.VMEM(coupling.shape[2:], jnp.float32),
            pltpu.VMEM((slots, links, width), jnp.int32),
            pltpu.VMEM(right_side.shape[2:], jnp.float32),
            pltpu.VMEM((slots, links, width), jnp.float32),
            pltpu.SemaphoreType.DMA((BUFFERS,)),
            pltpu.SemaphoreType.DMA((4,)),
        ],
        compiler_params=PARAMS,
        cost_estimate=LITTLE,
        name="prepare",
    )(info, flex, coupling, *in_place)
    mask, r, z, send, mine, other, prev_t, scatter = pl.pallas_call(
        functools.partial(first_kernel, corners, rows, levels),
        out_shape=(
            shape_of(slots, span), state, state, state, half_load, half_load, table(span, 2 * LANES),
            table(2 * LANES, coarse_size),
        ),
        in_specs=[SMEM] * 3 + [VMEM] * 6,
        out_specs=[VMEM] * 8,
        compiler_params=PARAMS,
        cost_estimate=LITTLE,
        name="first",
    )(info, partner, counts, right, weight, inverse, link_t, own_map, prev_coupling)

    def tables():
        return pl.pallas_call(
            functools.partial(table_kernel, rows, levels),
            out_shape=(table(2 * LANES, span), table(coarse_size, 2 * LANES), table(coarse_size, 2 * per_level)),
            in_specs=[SMEM] + [VMEM] * (2 + len(coarse_parts)),
            out_specs=[VMEM] * 3,
            scratch_shapes=[pltpu.VMEM((per_level, coarse_size), jnp.float32)],
            compiler_params=pltpu.CompilerParams(vmem_limit_bytes=max(14 * 1024 * 1024, 16 * per_level * coarse_size)),
            cost_estimate=LITTLE,
            name="tables",
        )(info, prev_coupling, own_map, *coarse_parts)

    kept = ()
    for iteration in range(ITERS):
        first, last = iteration == 0, iteration + 1 == ITERS
        forces = shifted(send, "col", -1)
        if first:
            forces, *coarse_parts[1:] = lax.optimization_barrier((forces, *coarse_parts[1:]))
            coarse_parts += [swapped(part, 1) for part in coarse_parts]
        total = mine + swapped(other, 1)
        if first:
            total = summed_along(total, level_bits)
            own, facing, energy, far_large, far_small = pl.pallas_call(
                flex_first_kernel,
                out_shape=(state, state, half_load) + half_pieces,
                in_specs=[VMEM] * 4 + [HBM],
                out_specs=[VMEM] * 5,
                scratch_shapes=[pltpu.VMEM((slots, loads, iface), jnp.float32)] + buffers + [pltpu.SemaphoreType.DMA((BUFFERS,))],
                compiler_params=PARAMS,
                cost_estimate=LITTLE,
                name="flex_first",
            )(z, forces, near_large, near_small, flex)
        else:
            total = summed_along(total, level_bits)
            own, facing, energy = pl.pallas_call(
                flex_kernel,
                out_shape=(state, state, half_load),
                in_specs=[VMEM] * 6,
                out_specs=[VMEM] * 3,
                compiler_params=PARAMS,
                cost_estimate=LITTLE,
                name="flex",
            )(z, forces, near_large, near_small, far_large, far_small)
        total = summed_along(total + energy, row_bits)
        rest = swapped(total, 1)
        facing_prev = shifted(facing, "col", 1)
        if first:
            prev, pick, coarse_table = tables()
        block = pl.pallas_call(
            functools.partial(coarse_kernel, rows, levels),
            out_shape=shape_of(loads // 2, 2 * per_level + LANES),
            in_specs=[SMEM] + [VMEM] * 3,
            out_specs=VMEM,
            compiler_params=PARAMS,
            cost_estimate=LITTLE,
            name="coarse",
        )(info, total, rest, coarse_table)
        blocks = gathered_along([block], level_bits)
        outs = (out_state, out_state) if last else (state,) * 5 + (small, state, half_load, half_load)
        results = pl.pallas_call(
            functools.partial(step_kernel, corners, levels, first, last),
            out_shape=outs,
            in_specs=[SMEM, SMEM] + [VMEM] * (14 + levels + len(kept)),
            out_specs=[VMEM] * len(outs),
            scratch_shapes=[pltpu.VMEM((slots, loads, span), jnp.float32)],
            compiler_params=PARAMS,
            cost_estimate=LITTLE,
            name="step",
        )(
            info, partner, own, facing_prev, weight, dof, inverse, mask, link, prev, link_t, prev_t,
            scatter, pick, r, z, *blocks, *kept,
        )
        if last:
            return results
        x, r, z, p, s, past, send, mine, other = results
        kept = (x, p, s, past)


def solution(mesh):
    in_specs = (
        P("row", "col", None, None, None),
        P("row", "col", None, None, None),
        P(("row", "col"), None),
        P("row", "col", None, None, None),
        P("row", "col", None, None, None, None),
        P("row", "col"),
        P("row", "col", None, None),
        P("row", "col", None, None, None),
        P("row", "col", None, None),
    )
    out_specs = (P("row", "col", None, None, None, None), P("row", "col", None, None, None, None))
    return jax.shard_map(local, mesh=mesh, in_specs=in_specs, out_specs=out_specs, check_vma=False)
```

```python
import functools
import jax
import jax.numpy as jnp
from jax import lax
from jax.experimental import pallas as pl
from jax.experimental.pallas import tpu as pltpu
from jax.sharding import PartitionSpec as P

ITERS = 3
BOTH = ("row", "col")
LANES = 128
BUFFERS = 6


def shifted(x, axis, by):
    devices = lax.axis_size(axis)
    return lax.ppermute(x, axis, [(i, (i + by) % devices) for i in range(devices)])


def swapped(x, bits):
    devices = lax.axis_size(BOTH)
    return lax.ppermute(x, BOTH, [(i, i ^ bits) for i in range(devices)])


def pieces(x, count):
    out = []
    for step in range(count):
        part = x.astype(jnp.bfloat16)
        out.append(part)
        if step + 1 < count:
            x = x - part.astype(jnp.float32)
    return out


def stacked(x, count):
    return jnp.concatenate(pieces(x, count), axis=0)


def matmul(a, b):
    return jnp.dot(a, b, preferred_element_type=jnp.float32)


def through_table(x, table):
    rows = x.shape[0]
    full = matmul(stacked(x, 2), table)
    return full[rows:] + full[:rows]


def slot_mask(slots, loads, corners):
    row = lax.broadcasted_iota(jnp.int32, (slots * loads, LANES), 0) // loads
    lane = lax.broadcasted_iota(jnp.int32, (slots * loads, LANES), 1) // corners
    return row == lane


def to_corners(values, columns, corners):
    slots, loads, n = values.shape
    rows = slots * loads
    full = matmul(stacked(values.reshape(rows, n), 2), columns)
    full = (full[rows:, :LANES] + full[:rows, LANES:]) + full[:rows, :LANES]
    kept = jnp.where(slot_mask(slots, loads, corners), full, 0.0)
    return jnp.sum(kept.reshape(slots, loads, LANES), axis=0)


def from_corners(answer, matrix, slots, corners):
    loads = answer.shape[0]
    rows = slots * loads
    spread = jnp.broadcast_to(answer[None], (slots, loads, LANES)).reshape(rows, LANES)
    spread = jnp.where(slot_mask(slots, loads, corners), spread, 0.0)
    both = stacked(spread, 2)
    full = matmul(jnp.concatenate([both, both], axis=1), matrix)
    return (full[rows:] + full[:rows]).reshape(slots, loads, full.shape[1])


def corner_rows(coupling, width):
    slots, corners, _ = coupling.shape
    parts = [coupling[s, :, :width] for s in range(slots)]
    if slots * corners < LANES:
        parts.append(jnp.zeros((LANES - slots * corners, width), jnp.float32))
    return jnp.concatenate(parts, axis=0)


def split_in_turn(flex_ref, part, large_ref, small_ref, buffer, sem):
    slots, iface = flex_ref.shape[2:4]
    depth = buffer.shape[1]
    per_slot = iface // 2 // depth
    chunks = slots * per_slot

    def chunk(c):
        first = pl.multiple_of(part * (iface // 2) + (c % per_slot) * depth, depth)
        return pltpu.make_async_copy(
            flex_ref.at[0, 0, c // per_slot, pl.ds(first, depth), :], buffer.at[c % BUFFERS], sem.at[c % BUFFERS]
        )

    def begin():
        for c in range(min(BUFFERS, chunks)):
            chunk(c).start()

    def one(c, carry):
        chunk(c).wait()
        rows = pl.ds(pl.multiple_of((c % per_slot) * depth, depth), depth)
        large, small = pieces(buffer[c % BUFFERS], 2)
        large_ref[c // per_slot, rows, :] = large
        small_ref[c // per_slot, rows, :] = small

        @pl.when(c + BUFFERS < chunks)
        def _():
            chunk(c + BUFFERS).start()

        return carry

    return begin, lambda slot, slots: lax.fori_loop(slot * per_slot, (slot + slots) * per_slot, one, 0)


def pack_kernel(coupling_ref, map_ref, counts_ref, out_ref, map_buffer, sem):
    slots, corners = coupling_ref.shape[2:4]
    span = out_ref.shape[1]
    copies = [
        pltpu.make_async_copy(
            coupling_ref.at[0, 0, s, :, pl.ds(span, span)], out_ref.at[pl.ds(s * corners, corners), :], sem.at[s]
        )
        for s in range(slots)
    ]
    maps = pltpu.make_async_copy(map_ref, map_buffer, sem.at[slots])
    maps.start()
    for copy in copies:
        copy.start()
    maps.wait()
    numbers = jnp.concatenate([map_buffer[s] for s in range(slots)], axis=0).astype(jnp.float32)
    numbers = jnp.concatenate([numbers, jnp.zeros((slots, LANES - corners), jnp.float32)], axis=1)
    live = jnp.full((slots, span - LANES), counts_ref[0, 0], jnp.int32).astype(jnp.float32)
    rest = out_ref.shape[0] - slots * corners - slots
    numbers = jnp.concatenate([jnp.concatenate([numbers, live], axis=1), jnp.zeros((rest, span), jnp.float32)], axis=0)
    out_ref[slots * corners :, :] = numbers
    for copy in copies:
        copy.wait()


def without_numbers(packed, used):
    row = lax.broadcasted_iota(jnp.int32, packed.shape, 0)
    return jnp.where(row < used, packed, 0.0)


def prepare_kernel(
    info_ref, flex_ref, coupling_ref, dof_ref, right_ref, weight_ref, large_ref, small_ref, inverse_ref, dof_rows_ref, link_ref,
    link_t_ref, right_rows_ref, weight_rows_ref, buffer, coupling_buffer, dof_buffer, right_buffer, weight_buffer, flex_sem, sem,
):
    slots, links, width = dof_buffer.shape
    span = links * width
    begin, end = split_in_turn(flex_ref, 0, large_ref, small_ref, buffer, flex_sem)
    others = [
        pltpu.make_async_copy(dof_ref.at[0, 0], dof_buffer, sem.at[0]),
        pltpu.make_async_copy(coupling_ref.at[0, 0], coupling_buffer, sem.at[1]),
        pltpu.make_async_copy(right_ref.at[0, 0], right_buffer, sem.at[2]),
        pltpu.make_async_copy(weight_ref.at[0, 0], weight_buffer, sem.at[3]),
    ]
    for copy in others:
        copy.start()
    begin()
    others[0].wait()
    for j in range(slots):
        for k in range(links):
            at = slice(j * links + k, j * links + k + 1)
            met = dof_buffer[j, k : k + 1, :]
            hit = jnp.broadcast_to(met, (width, width)) == lax.broadcasted_iota(jnp.int32, (width, width), 0)
            place = jnp.where(hit, lax.broadcasted_iota(jnp.int32, (width, width), 1), 0).astype(jnp.float32)
            found = jnp.sum(place.T, axis=0, keepdims=True)
            inverse_ref[at, :] = found.astype(jnp.int32)
            dof_rows_ref[at, :] = met
    end(0, 2)
    others[1].wait()
    link = corner_rows(coupling_buffer[...], span)
    link_ref[...] = stacked(link, 2)
    link_t_ref[...] = jnp.concatenate(pieces(link.T, 2), axis=1)
    end(2, 1)
    others[2].wait()
    others[3].wait()
    for j in range(slots):
        for k in range(links):
            lanes = slice(k * width, (k + 1) * width)
            right_rows_ref[j, :, lanes] = right_buffer[j, :, k, :]
            weight_rows_ref[j : j + 1, lanes] = weight_buffer[j, k : k + 1, :]
    end(3, slots - 3)


def beside(x):
    half = x.shape[0] // 2
    return jnp.concatenate([x[:half], x[half:]], axis=1)


def stacked_again(x):
    half = x.shape[1] // 2
    return jnp.concatenate([x[:, :half], x[:, half:]], axis=0)


def lane_pair(column, at):
    half = column.shape[0] // 2
    lane = lax.broadcasted_iota(jnp.int32, (half, LANES), 1)
    return jnp.where(lane == at, column[:half], jnp.where(lane == at + 1, column[half:], 0.0))


def column_of(tile, at):
    return jnp.concatenate([tile[:, at : at + 1], tile[:, at + 1 : at + 2]], axis=0)


def start_exchange(
    z, norm, partner_ref, inverse_ref, link_t_ref, prev_t_ref, scatter_ref, parity, corners, send_ref, mine_ref, other_ref
):
    slots, loads, span = z.shape
    links = span // LANES
    for j in range(slots):
        for k in range(links):
            block = z[j, :, k * LANES : (k + 1) * LANES]
            index = jnp.broadcast_to(inverse_ref[j * links + k][None], (loads, LANES))
            send_ref[partner_ref[0, 0, k, j], :, k * LANES : (k + 1) * LANES] = -jnp.take_along_axis(block, index, axis=1)
    own = to_corners(z, link_t_ref[...], corners)
    prev = to_corners(send_ref[...], prev_t_ref[...], corners)
    load = through_table(jnp.concatenate([own, prev], axis=1), scatter_ref[...])
    half = load.shape[1] // 2
    low, high = beside(load[:, :half]), beside(load[:, half:])
    spare = lane_pair(norm, 0)
    mine_ref[:, : 2 * half] = jnp.where(parity == 0, low, high)
    other_ref[:, : 2 * half] = jnp.where(parity == 0, high, low)
    mine_ref[:, 2 * half :] = spare
    other_ref[:, 2 * half :] = spare


def local_norm(r, z):
    return jnp.sum(jnp.sum(r * z, axis=0), axis=1, keepdims=True)


def by_level(numbers, rows, levels):
    row = numbers // (2 * rows * levels)
    rest = numbers - row * (2 * rows * levels)
    level = rest // (2 * rows)
    return level, row * (2 * rows) + rest - level * (2 * rows)


def first_kernel(
    corners, rows, levels, info_ref, partner_ref, counts_ref, right_ref, weight_ref, inverse_ref, link_t_ref, map_ref, prev_ref,
    mask_ref, r_ref, z_ref, send_ref, mine_ref, other_ref, prev_t_ref, scatter_ref,
):
    slots, loads, span = r_ref.shape
    links = span // LANES
    used = slots * corners
    live_prev = prev_ref[used : used + 1, LANES : LANES + 1]
    for j in range(slots):
        live = jnp.where(j < counts_ref[0, 0], live_prev, 0.0)
        for k in range(links):
            met = jnp.full((1, LANES), partner_ref[0, 0, k, j], jnp.int32).astype(jnp.float32)
            mask_ref[j : j + 1, k * LANES : (k + 1) * LANES] = jnp.where(met < live, 1.0, 0.0)
    r = right_ref[...] * mask_ref[...][:, None, :]
    z = weight_ref[...][:, None, :] * r
    r_ref[...] = r
    z_ref[...] = z
    prev_t_ref[...] = jnp.concatenate(pieces(without_numbers(prev_ref[...], used).T, 2), axis=1)
    size = scatter_ref.shape[1]
    lane = lax.broadcasted_iota(jnp.int32, (corners, size), 1)
    own = jnp.concatenate([map_ref[j] for j in range(slots)], axis=0).astype(jnp.float32)
    own = jnp.concatenate([own, jnp.zeros((slots, LANES - corners), jnp.float32)], axis=1)
    both = jnp.concatenate([own, prev_ref[used : used + slots, :LANES]], axis=0)
    both = jnp.concatenate([both, jnp.zeros((16 - 2 * slots, LANES), jnp.float32)], axis=0)
    level, within = by_level(both.astype(jnp.int32), rows, levels)
    both = (level * (size // levels) + within).astype(jnp.float32).T
    own = [both[:corners, j : j + 1] for j in range(slots)]
    prev = [both[:corners, slots + j : slots + j + 1] for j in range(slots)]
    for side, columns in enumerate((own, prev)):
        parts = [(c.astype(jnp.int32) == lane).astype(jnp.float32) for c in columns]
        if slots * corners < LANES:
            parts.append(jnp.zeros((LANES - slots * corners, size), jnp.float32))
        scatter_ref[side * LANES : (side + 1) * LANES, :] = jnp.concatenate(parts, axis=0).astype(jnp.bfloat16)
    start_exchange(
        z, local_norm(r, z), partner_ref, inverse_ref, link_t_ref, prev_t_ref, scatter_ref, info_ref[0], corners,
        send_ref, mine_ref, other_ref,
    )


def table_kernel(rows, levels, info_ref, packed_ref, map_ref, *refs):
    *parts, prev_ref, pick_ref, coarse_ref, joined_ref = refs
    slots, _, corners = map_ref.shape
    used = slots * corners
    prev_ref[...] = stacked(without_numbers(packed_ref[...], used), 2)
    side_rows = len(parts) // 2
    per_level = rows * len(parts)
    lines = []
    own = [map_ref[s] for s in range(slots)]
    prev = [packed_ref[used + s : used + s + 1, :corners].astype(jnp.int32) for s in range(slots)]
    for line in (own, prev):
        if slots * corners < LANES:
            line.append(jnp.full((1, LANES - slots * corners), -1, jnp.int32))
        lines += line
    maps = jnp.concatenate(lines, axis=1)
    level, within = by_level(maps, rows, levels)
    place = jnp.bitwise_xor(level, info_ref[2]) * per_level + within
    place = jnp.where(maps >= 0, place, -1)
    pick_ref[...] = (place == lax.broadcasted_iota(jnp.int32, pick_ref.shape, 0)).astype(jnp.bfloat16)
    for core in range(2):
        for away in range(side_rows):
            at = jnp.bitwise_xor(info_ref[1], away) * (2 * rows) + jnp.bitwise_xor(info_ref[0], core) * rows
            joined_ref[pl.ds(pl.multiple_of(at, 8), rows), :] = parts[core * side_rows + away][...]
    turned = jnp.concatenate(pieces(joined_ref[...].T, 2), axis=1)
    stretch = 2 * rows
    for at in range(side_rows):
        for level in range(levels):
            source = (at * levels + level) * stretch
            target = level * per_level + at * stretch
            coarse_ref[target : target + stretch, :] = turned[source : source + stretch]


def step_kernel(
    corners, levels, first, last, info_ref, partner_ref, own_ref, facing_ref, weight_ref, dof_ref,
    inverse_ref, mask_ref, link_ref, prev_ref, link_t_ref, prev_t_ref, scatter_ref, pick_ref, r_ref, z_ref, *refs,
):
    refs = list(refs)
    block_refs = refs[:levels]
    refs = refs[levels:]
    if not first:
        x_ref, p_ref, s_ref, past_ref = refs[:4]
        refs = refs[4:]
    x_out, r_out = refs[:2]
    far_ref = refs[-1]
    slots, loads, span = own_ref.shape
    links = span // LANES
    per_level = pick_ref.shape[0] // levels
    spare = block_refs[0][:, 2 * per_level :]
    norm = column_of(spare, 2)
    for ref in block_refs[1:]:
        spare = spare + ref[:, 2 * per_level :]
    product = column_of(spare, 0)
    gathered = jnp.concatenate([stacked_again(ref[:, : 2 * per_level]) for ref in block_refs], axis=1)
    picked = through_table(gathered, pick_ref[...])
    near = own_ref[...] + from_corners(picked[:, :LANES], link_ref[...], slots, corners)
    far_ref[...] = facing_ref[...] + from_corners(picked[:, LANES:], prev_ref[...], slots, corners)
    jumps = []
    for j in range(slots):
        parts = []
        for k in range(links):
            block = far_ref[partner_ref[0, 0, k, j], :, k * LANES : (k + 1) * LANES]
            index = jnp.broadcast_to(dof_ref[j * links + k][None], (loads, LANES))
            parts.append(jnp.take_along_axis(block, index, axis=1))
        jumps.append(jnp.concatenate(parts, axis=1)[None])
    image = (near - jnp.concatenate(jumps, axis=0)) * mask_ref[...][:, None, :]
    if first:
        alpha = norm / product
        p, s = z_ref[...], image
        x = alpha[None] * p
    else:
        ratio = norm / past_ref[:, :1]
        alpha = norm / (product - ratio * norm / past_ref[:, 1:2])
        p = z_ref[...] + ratio[None] * p_ref[...]
        s = image + ratio[None] * s_ref[...]
        x = x_ref[...] + alpha[None] * p
    r = r_ref[...] - alpha[None] * s
    if last:
        for j in range(slots):
            for k in range(links):
                x_out[0, 0, j, :, k, :] = x[j, :, k * LANES : (k + 1) * LANES]
                r_out[0, 0, j, :, k, :] = r[j, :, k * LANES : (k + 1) * LANES]
        return
    z_out, p_out, s_out, past_out, send_ref, mine_ref, other_ref = refs[2:9]
    x_out[...] = x
    r_out[...] = r
    z = weight_ref[...][:, None, :] * r
    z_out[...] = z
    p_out[...] = p
    s_out[...] = s
    lane = lax.broadcasted_iota(jnp.int32, past_out.shape, 1)
    past_out[...] = jnp.where(lane == 0, norm, alpha)
    start_exchange(
        z, local_norm(r, z), partner_ref, inverse_ref, link_t_ref, prev_t_ref, scatter_ref, info_ref[0], corners,
        send_ref, mine_ref, other_ref,
    )


def flex_product(values, large, small):
    loads = values.shape[0]
    full = matmul(stacked(values, 2), large)
    rest = matmul(values.astype(jnp.bfloat16), small)
    return (full[loads:] + rest) + full[:loads]


def flex_near_kernel(values_ref, large_ref, small_ref, out_ref):
    slots, _, width = values_ref.shape
    for s in range(slots):
        out_ref[s] = flex_product(values_ref[s], large_ref[s], small_ref[s])


def flex_far_slot(s, begun, values_ref, forces_ref, large_ref, small_ref, own_ref, facing_ref):
    width = values_ref.shape[2]
    answer = begun + flex_product(forces_ref[s], large_ref[s], small_ref[s])
    own, facing = answer[:, :width], answer[:, width:]
    own_ref[s] = own
    facing_ref[s] = facing
    return jnp.sum(values_ref[s] * own + forces_ref[s] * facing, axis=1, keepdims=True)


def write_energy(work, energy_ref):
    half = energy_ref.shape[1] - LANES
    energy_ref[:, :half] = jnp.zeros((energy_ref.shape[0], half), jnp.float32)
    energy_ref[:, half:] = lane_pair(work, 2)


def flex_kernel(
    values_ref, forces_ref, near_large_ref, near_small_ref, large_ref, small_ref, own_ref, facing_ref, energy_ref
):
    slots, loads, _ = values_ref.shape
    work = jnp.zeros((loads, 1), jnp.float32)
    for s in range(slots):
        begun = flex_product(values_ref[s], near_large_ref[s], near_small_ref[s])
        work += flex_far_slot(s, begun, values_ref, forces_ref, large_ref, small_ref, own_ref, facing_ref)
    write_energy(work, energy_ref)


def flex_first_kernel(
    values_ref, forces_ref, near_large_ref, near_small_ref, flex_ref, own_ref, facing_ref, energy_ref, large_ref, small_ref,
    begun_ref, buffer, sem,
):
    slots, loads, _ = values_ref.shape
    begin, end = split_in_turn(flex_ref, 1, large_ref, small_ref, buffer, sem)
    begin()
    flex_near_kernel(values_ref, near_large_ref, near_small_ref, begun_ref)
    work = jnp.zeros((loads, 1), jnp.float32)
    for s in range(slots):
        end(s, 1)
        work += flex_far_slot(s, begun_ref[s], values_ref, forces_ref, large_ref, small_ref, own_ref, facing_ref)
    write_energy(work, energy_ref)


def coarse_kernel(rows, levels, info_ref, mine_ref, other_ref, table_ref, out_ref):
    parity = info_ref[0]
    half = mine_ref.shape[1] - LANES
    mine, other = stacked_again(mine_ref[:, :half]), stacked_again(other_ref[:, :half])
    low, high = jnp.where(parity == 0, mine, other), jnp.where(parity == 0, other, mine)
    load = jnp.concatenate([low, high], axis=1)
    loads, size = load.shape
    per_level = table_ref.shape[1] // 2
    full = matmul(stacked(load, 2), table_ref[...])

    def part(i, j):
        return full[i * loads : (i + 1) * loads, j * per_level : (j + 1) * per_level]

    answer = (part(1, 1) + (part(1, 0) + part(0, 1))) + part(0, 0)
    own = load[:, :per_level]
    for level in range(1, levels):
        own = jnp.where(info_ref[2] == level, load[:, level * per_level : (level + 1) * per_level], own)
    spare = mine_ref[:, half:]
    product = jnp.sum(answer * own, axis=1, keepdims=True) + column_of(spare + other_ref[:, half:], 2)
    out_ref[:, : 2 * per_level] = beside(answer)
    out_ref[:, 2 * per_level :] = lane_pair(product, 0) + lane_pair(column_of(spare, 0), 2)


VMEM = pl.BlockSpec(memory_space=pltpu.VMEM)
SMEM = pl.BlockSpec(memory_space=pltpu.SMEM)
HBM = pl.BlockSpec(memory_space=pltpu.HBM)
LITTLE = pl.CostEstimate(flops=1024, bytes_accessed=1024, transcendentals=0)
PARAMS = pltpu.CompilerParams(vmem_limit_bytes=14 * 1024 * 1024)


def shape_of(*dims, dtype=jnp.float32):
    return pltpu.VMEM(dims, dtype)


def gathered_along(blocks, bits):
    if len(bits) == 2 and len(blocks) == 1:
        return blocks + [swapped(blocks[0], b) for b in (bits[0], bits[1], bits[0] + bits[1])]
    for bit in bits:
        blocks = blocks + [swapped(b, bit) for b in blocks]
    return blocks


def summed_along(total, bits):
    if len(bits) == 2:
        return sum([swapped(total, b) for b in (bits[0], bits[1], bits[0] + bits[1])], total)
    for bit in bits:
        total = total + swapped(total, bit)
    return total


def powers(start, stop):
    out = []
    while start < stop:
        out.append(start)
        start *= 2
    return out


def local(
    flexibility,
    coupling,
    coarse_inverse,
    precon_weight,
    right_side,
    counts,
    partner,
    dof_index,
    corner_map,
):
    devices, columns = lax.axis_size(BOTH), lax.axis_size("col")
    levels = columns // 2
    slots, iface = flexibility.shape[2:4]
    links, width = dof_index.shape[-2:]
    loads = right_side.shape[3]
    corners = corner_map.shape[-1]
    rows, coarse_size = coarse_inverse.shape
    span = links * width
    per_level = coarse_size // levels
    row_bits, level_bits = powers(columns, devices), powers(2, columns)
    at_col = lax.axis_index("col")
    info = jnp.stack([at_col % 2, lax.axis_index("row"), at_col // 2]).astype(jnp.int32)

    own_map = corner_map.reshape(slots, 1, corners)
    coupling = pltpu.with_memory_space_constraint(coupling, pltpu.HBM)
    to_next = pl.pallas_call(
        pack_kernel,
        out_shape=shape_of(LANES, span),
        in_specs=[HBM, HBM, SMEM],
        out_specs=VMEM,
        scratch_shapes=[pltpu.VMEM((slots, 1, corners), jnp.int32), pltpu.SemaphoreType.DMA((slots + 1,))],
        compiler_params=PARAMS,
        cost_estimate=LITTLE,
        name="pack",
    )(coupling, pltpu.with_memory_space_constraint(own_map, pltpu.HBM), counts)
    coarse_inverse, to_next = lax.optimization_barrier((coarse_inverse, to_next))
    prev_coupling = shifted(to_next, "col", 1)
    coarse_parts = gathered_along([coarse_inverse], row_bits)

    state = shape_of(slots, loads, span)
    small = shape_of(loads, LANES)
    half_load = shape_of(loads // 2, coarse_size + LANES)
    out_state = jax.ShapeDtypeStruct(right_side.shape, jnp.float32)

    def table(*dims):
        return shape_of(*dims, dtype=jnp.bfloat16)

    depth = iface // 4
    half_pieces = (table(slots, span, iface), table(slots, span, iface))
    buffers = [pltpu.VMEM((BUFFERS, depth, iface), jnp.float32)]
    flex = pltpu.with_memory_space_constraint(flexibility, pltpu.HBM)
    in_place = [pltpu.with_memory_space_constraint(a, pltpu.HBM) for a in (dof_index, right_side, precon_weight)]
    near_large, near_small, inverse, dof, link, link_t, right, weight = pl.pallas_call(
        prepare_kernel,
        out_shape=half_pieces
        + (
            shape_of(slots * links, width, dtype=jnp.int32), shape_of(slots * links, width, dtype=jnp.int32),
            table(2 * LANES, span), table(span, 2 * LANES), state, shape_of(slots, span),
        ),
        in_specs=[SMEM] + [HBM] * 5,
        out_specs=[VMEM] * 8,
        scratch_shapes=buffers
        + [
            pltpu.VMEM(coupling.shape[2:], jnp.float32),
            pltpu.VMEM((slots, links, width), jnp.int32),
            pltpu.VMEM(right_side.shape[2:], jnp.float32),
            pltpu.VMEM((slots, links, width), jnp.float32),
            pltpu.SemaphoreType.DMA((BUFFERS,)),
            pltpu.SemaphoreType.DMA((4,)),
        ],
        compiler_params=PARAMS,
        cost_estimate=LITTLE,
        name="prepare",
    )(info, flex, coupling, *in_place)
    mask, r, z, send, mine, other, prev_t, scatter = pl.pallas_call(
        functools.partial(first_kernel, corners, rows, levels),
        out_shape=(
            shape_of(slots, span), state, state, state, half_load, half_load, table(span, 2 * LANES),
            table(2 * LANES, coarse_size),
        ),
        in_specs=[SMEM] * 3 + [VMEM] * 6,
        out_specs=[VMEM] * 8,
        compiler_params=PARAMS,
        cost_estimate=LITTLE,
        name="first",
    )(info, partner, counts, right, weight, inverse, link_t, own_map, prev_coupling)

    def tables():
        return pl.pallas_call(
            functools.partial(table_kernel, rows, levels),
            out_shape=(table(2 * LANES, span), table(coarse_size, 2 * LANES), table(coarse_size, 2 * per_level)),
            in_specs=[SMEM] + [VMEM] * (2 + len(coarse_parts)),
            out_specs=[VMEM] * 3,
            scratch_shapes=[pltpu.VMEM((per_level, coarse_size), jnp.float32)],
            compiler_params=pltpu.CompilerParams(vmem_limit_bytes=max(14 * 1024 * 1024, 16 * per_level * coarse_size)),
            cost_estimate=LITTLE,
            name="tables",
        )(info, prev_coupling, own_map, *coarse_parts)

    kept = ()
    for iteration in range(ITERS):
        first, last = iteration == 0, iteration + 1 == ITERS
        forces = shifted(send, "col", -1)
        if first:
            forces, *coarse_parts[1:] = lax.optimization_barrier((forces, *coarse_parts[1:]))
            coarse_parts += [swapped(part, 1) for part in coarse_parts]
        total = mine + swapped(other, 1)
        if first:
            total = summed_along(total, level_bits)
            own, facing, energy, far_large, far_small = pl.pallas_call(
                flex_first_kernel,
                out_shape=(state, state, half_load) + half_pieces,
                in_specs=[VMEM] * 4 + [HBM],
                out_specs=[VMEM] * 5,
                scratch_shapes=[pltpu.VMEM((slots, loads, iface), jnp.float32)] + buffers + [pltpu.SemaphoreType.DMA((BUFFERS,))],
                compiler_params=PARAMS,
                cost_estimate=LITTLE,
                name="flex_first",
            )(z, forces, near_large, near_small, flex)
        else:
            total = summed_along(total, level_bits)
            own, facing, energy = pl.pallas_call(
                flex_kernel,
                out_shape=(state, state, half_load),
                in_specs=[VMEM] * 6,
                out_specs=[VMEM] * 3,
                compiler_params=PARAMS,
                cost_estimate=LITTLE,
                name="flex",
            )(z, forces, near_large, near_small, far_large, far_small)
        total = summed_along(total + energy, row_bits)
        rest = swapped(total, 1)
        facing_prev = shifted(facing, "col", 1)
        if first:
            prev, pick, coarse_table = tables()
        block = pl.pallas_call(
            functools.partial(coarse_kernel, rows, levels),
            out_shape=shape_of(loads // 2, 2 * per_level + LANES),
            in_specs=[SMEM] + [VMEM] * 3,
            out_specs=VMEM,
            compiler_params=PARAMS,
            cost_estimate=LITTLE,
            name="coarse",
        )(info, total, rest, coarse_table)
        blocks = gathered_along([block], level_bits)
        outs = (out_state, out_state) if last else (state,) * 5 + (small, state, half_load, half_load)
        results = pl.pallas_call(
            functools.partial(step_kernel, corners, levels, first, last),
            out_shape=outs,
            in_specs=[SMEM, SMEM] + [VMEM] * (14 + levels + len(kept)),
            out_specs=[VMEM] * len(outs),
            scratch_shapes=[pltpu.VMEM((slots, loads, span), jnp.float32)],
            compiler_params=PARAMS,
            cost_estimate=LITTLE,
            name="step",
        )(
            info, partner, own, facing_prev, weight, dof, inverse, mask, link, prev, link_t, prev_t,
            scatter, pick, r, z, *blocks, *kept,
        )
        if last:
            return results
        x, r, z, p, s, past, send, mine, other = results
        kept = (x, p, s, past)


def solution(mesh):
    in_specs = (
        P("row", "col", None, None, None),
        P("row", "col", None, None, None),
        P(("row", "col"), None),
        P("row", "col", None, None, None),
        P("row", "col", None, None, None, None),
        P("row", "col"),
        P("row", "col", None, None),
        P("row", "col", None, None, None),
        P("row", "col", None, None),
    )
    out_specs = (P("row", "col", None, None, None, None), P("row", "col", None, None, None, None))
    return jax.shard_map(local, mesh=mesh, in_specs=in_specs, out_specs=out_specs, check_vma=False)
```
